32 devices in a mesh: parts: 2 (over y), seq: 4 (over z), chan: 4 (over x, core).
Axes of the slice: x: 2, y: 2, z: 4, core: 2. Of those that a mesh axis runs over, the one named last changes fastest.
Arguments:
- x_tokens: bfloat16 [64, 8192], P(('parts', 'seq'), 'chan'), parts along dimension 0, may hold values from -6 to 6
- norm_gain: float32 [8192], P('chan'), may hold values from 0.5 to 1.5
- w_in: bfloat16 [3, 8192, 8192], P(None, 'seq', 'chan'), may hold values from -0.0625 to 0.0625
- short_filter: float32 [3, 3, 8192], P(None, None, 'seq'), may hold values from -3 to 3
- se_filter: float32 [7, 512], P(None, 'seq'), may hold values from -2 to 2
- w_out: bfloat16 [8192, 8192], P('seq'), may hold values from -0.0625 to 0.0625
Outputs:
- mixed_out: bfloat16 [64, 8192], P(('parts', 'chan'), 'seq'), parts along dimension 0
The draws below stay inside these ranges and needn't reach their ends.
There are 2 independent parts, one for each index of `parts`. The reference program is written for one: setup_inputs(seed, part) draws one part's arguments, and reference() takes and returns one part's arrays. A program takes and returns all parts, laid end to end along the dimension named above; an argument that names none is the same for every part. Nothing has to cross between parts.
All inputs are finite; a program needn't handle non-finite values.
Results may differ from the reference program's by a relative error of at most 0.0086.
Values may be sent and summed in bfloat16 or wider, within the bound.
A program may use at most 128 MiB of HBM per device.

```python
import jax
import jax.numpy as jnp
from jax import lax

D = 8192
GROUP = 16
TOKENS = 32
FILTERS = 512


def block_levels(stream_key, extent, shards, smallest, top_value):
    def one(dim, shards_of):
        draws = jax.random.uniform(jax.random.fold_in(jax.random.fold_in(stream_key, 6), dim), (shards_of,), jnp.float32, smallest / len(shards), top_value / len(shards))
        return jnp.repeat(jnp.exp(draws), extent[dim] // shards_of).reshape((-1,) + (1,) * (len(extent) - dim - 1))

    loudness = one(*shards[0])
    for cut in shards[1:]:
        loudness = loudness * one(*cut)
    return loudness


def noise(key, extent, spread, bound, pieces=(), dtype=jnp.bfloat16):
    values = jax.random.normal(key, extent, jnp.float32) * spread
    if len(pieces) > 0:
        values = block_levels(key, extent, pieces, -0.22, 0.18) * values
    return jnp.clip(values, min=-bound, max=bound).astype(dtype)


def setup_inputs(seed: int = 0, part: int = 0) -> dict:
    seeds = jax.random.split(jax.random.key(seed), 7)
    own_keys = jax.random.split(jax.random.fold_in(seeds[6], part), 7)
    x_tokens = noise(own_keys[0], (TOKENS, D), 1.0, 6.0, ((0, 4), (1, 4)))
    norm_gain = jnp.clip(1.0 + 0.1 * jax.random.normal(seeds[1], (D,), jnp.float32), 0.5, 1.5)
    w_in = noise(seeds[2], (3, D, D), D ** -0.5, 0.0625, ((1, 4), (2, 4)))
    short_filter = noise(seeds[3], (3, 3, D), 0.6, 3.0, ((2, 4),), jnp.float32)
    se_filter = noise(seeds[4], (7, FILTERS), 0.4, 2.0, ((1, 4),), jnp.float32)
    w_out = noise(seeds[5], (D, D), D ** -0.5, 0.0625, ((0, 4),))
    return {"x_tokens": x_tokens, "norm_gain": norm_gain, "w_in": w_in, "short_filter": short_filter, "se_filter": se_filter, "w_out": w_out}


epsilon = 1e-06

def rms_normalize(rows, gain):
    wide = rows.astype(jnp.float32)
    factor = lax.rsqrt(lax.optimization_barrier(jnp.mean(wide * wide, axis=-1, keepdims=True)) + epsilon)
    return (wide * factor * gain).astype(jnp.bfloat16)

def mixer(extended, short_taps, long_taps):
    wide = extended.astype(jnp.float32)
    row_count = wide.shape[0]
    featured = sum((short_taps[offset] * wide[2 - offset:row_count - offset] for offset in range(3)))
    queries = featured[:, 0]
    product = featured[:, 1] * featured[:, 2]
    length = product.shape[0]
    filtered = sum((long_taps[offset] * product[6 - offset:length - offset] for offset in range(7)))
    return (queries[6:] * filtered).astype(jnp.bfloat16)

def reference(x_tokens, norm_gain, w_in, short_filter, se_filter, w_out):
    normed = rms_normalize(x_tokens, norm_gain)
    flat_in = w_in.reshape(3 * D, D)
    projected = lax.dot_general(normed, flat_in, (((1,), (1,)), ((), ())), preferred_element_type=jnp.float32).astype(jnp.bfloat16)
    projected = projected.reshape(TOKENS, 3, D)
    extended = jnp.concatenate([jnp.zeros((8, 3, D), jnp.bfloat16), projected], axis=0)
    gated = mixer(extended, short_filter, jnp.repeat(se_filter, GROUP, axis=1))
    mixed = lax.dot_general(gated, w_out, (((1,), (1,)), ((), ())), preferred_element_type=jnp.float32)
    return mixed.astype(jnp.bfloat16)
```

```python
import functools

import jax
import jax.numpy as jnp
from jax import lax
from jax.experimental import pallas as pl
from jax.experimental.pallas import tpu as pltpu
from jax.sharding import PartitionSpec as P

D = 8192
GROUP = 16
MIB = 2**20


epsilon = 1e-06


def from_behind(value, axis, steps):
    count = lax.axis_size(axis)
    leading, last = (max(0, -steps), min(count, count - steps))
    return lax.ppermute(value, axis, [(source, source + steps) for source in range(leading, last)])


def mixer(extended, short_taps, long_taps):
    wide = extended.astype(jnp.float32)
    row_count = wide.shape[0]
    featured = sum(
        (short_taps[offset] * wide[2 - offset : row_count - offset] for offset in range(3))
    )
    queries = featured[:, 0]
    product = featured[:, 1] * featured[:, 2]
    length = product.shape[0]
    filtered = sum(
        (long_taps[offset] * product[6 - offset : length - offset] for offset in range(7))
    )
    return (queries[6:] * filtered).astype(jnp.bfloat16)


def contract_last(left, right):
    return lax.dot_general(
        left, right, (((1,), (1,)), ((), ())), preferred_element_type=jnp.float32
    )


def plain(x_tokens, norm_gain, w_in, short_filter, se_filter, w_out):
    wide = x_tokens.astype(jnp.float32)
    local_squares = jnp.sum(wide * wide, axis=1, keepdims=True)
    total_squares = lax.psum(local_squares, "chan")
    factor = lax.rsqrt(total_squares / D + epsilon)
    normed = (wide * factor * norm_gain).astype(jnp.bfloat16)
    columns = w_in.shape[1]
    flat_in = w_in.reshape(3 * columns, w_in.shape[2])
    piece = lax.all_gather(normed, "seq", axis=0, tiled=True)
    partial_terms = contract_last(piece, flat_in).reshape(piece.shape[0], 3, columns)
    long_full = jnp.repeat(se_filter, GROUP, axis=1)
    mine = lax.psum_scatter(partial_terms, "chan", scatter_dimension=0, tiled=True).astype(
        jnp.bfloat16
    )
    previous = from_behind(mine[-8:], "chan", 1)
    extended = jnp.concatenate([previous, mine], axis=0)
    gated = mixer(extended, short_filter, long_full)
    result = contract_last(lax.all_gather(gated, "seq", axis=1, tiled=True), w_out)
    return result.astype(jnp.bfloat16)


def partners(me, count):
    if count % 2:
        return [lax.rem(me + step, count) for step in range(1, count)]
    chip, core, chips = me // 2, lax.rem(me, 2), count // 2
    found = []
    for step in range(1, chips):
        other = 2 * lax.rem(chip + step, chips)
        found += [other + core, other + 1 - core]
    return found + [2 * chip + 1 - core]


def delayed(value, steps):
    if steps == 0:
        return value
    tokens = lax.broadcasted_iota(jnp.int32, value.shape, 0)
    return jnp.where(tokens >= steps, pltpu.roll(value, steps, 0), 0.0)


def kernel(
    seqs, chans,
    x_hbm, gain_hbm, w_in_hbm, short_hbm, se_hbm, w_out_hbm, out_ref,
    xs, gain, w_in, short, se, w_out, normed, squares, factors, stage, landed, own, gathered, total,
    leaving, arriving,
    small_sem, w_in_sem, w_out_sem, x_send, x_recv, sq_send, sq_recv, f_send, f_recv, p_send, p_recv,
    g_send, g_recv, o_send, o_recv,
):
    seq, chan = lax.axis_index("seq"), lax.axis_index("chan")
    tokens, block = own.shape[1:]
    columns, features = w_out.shape[1], w_in.shape[3]
    rows = out_ref.shape[0]
    seq_others = [lax.rem(seq + step, seqs) for step in range(1, seqs)]
    chan_others = partners(chan, chans)

    def send(source, target, send_sem, recv_sem, axis, index):
        copy = pltpu.make_async_remote_copy(
            src_ref=source, dst_ref=target, send_sem=send_sem, recv_sem=recv_sem,
            device_id={axis: index}, device_id_type=pl.DeviceIdType.MESH,
        )
        copy.start()
        return copy

    def local(source, target, sem):
        copy = pltpu.make_async_copy(source, target, sem)
        copy.start()
        return copy

    def arrived(target, sem):
        pltpu.make_async_copy(target, target, sem).wait()

    x_copy = local(x_hbm, xs.at[seq], small_sem.at[0])
    gain_copy = local(gain_hbm, gain, small_sem.at[1])
    short_copy = local(short_hbm, short, small_sem.at[2])
    se_copy = local(se_hbm, se, small_sem.at[3])
    w_in_copies = []
    for step, index in enumerate(chan_others + [chan]):
        span = pl.ds(pl.multiple_of(index * block, block), block)
        w_in_copies.append([
            local(w_in_hbm.at[part, span], w_in.at[step, part], w_in_sem.at[step, part])
            for part in range(3)
        ])
    w_out_copies = []
    for step, index in enumerate([seq] + seq_others):
        span = pl.ds(pl.multiple_of(index * columns + chan * block, block), block)
        w_out_copies.append(local(w_out_hbm.at[:, span], w_out.at[step], w_out_sem.at[step]))

    barrier = pltpu.get_barrier_semaphore()
    for axis, others in (("seq", seq_others), ("chan", chan_others)):
        for index in others:
            pl.semaphore_signal(
                barrier, inc=1, device_id={axis: index}, device_id_type=pl.DeviceIdType.MESH
            )
    x_copy.wait()
    pl.semaphore_wait(barrier, seqs + chans - 2)

    sent = [
        send(xs.at[seq], xs.at[seq], x_send.at[step], x_recv.at[seq], "seq", index)
        for step, index in enumerate(seq_others)
    ]

    wide = xs[seq].astype(jnp.float32)
    squares[chan] = jnp.broadcast_to(
        jnp.sum(wide * wide, axis=1, keepdims=True), squares.shape[1:]
    )
    sent += [
        send(squares.at[chan], squares.at[chan], sq_send.at[step], sq_recv.at[chan], "chan", index)
        for step, index in enumerate(chan_others)
    ]
    for index in chan_others:
        arrived(squares.at[index], sq_recv.at[index])
    factors[seq] = lax.rsqrt(jnp.sum(squares[...], axis=0) / (features * chans) + epsilon)
    sent += [
        send(factors.at[seq], factors.at[seq], f_send.at[step], f_recv.at[seq], "seq", index)
        for step, index in enumerate(seq_others)
    ]

    se_copy.wait()
    short_copy.wait()
    gain_copy.wait()
    filters = se.shape[1]
    group = columns // filters
    first = lax.broadcasted_iota(jnp.int32, (filters, block), 0) * group
    channel = lax.broadcasted_iota(jnp.int32, (filters, block), 1) + chan * block
    spread = jnp.where((channel >= first) & (channel < first + group), 1.0, 0.0)
    long_taps = jnp.dot(
        se[...], spread, preferred_element_type=jnp.float32, precision=lax.Precision.HIGHEST
    )

    for index in seq_others:
        arrived(factors.at[index], f_recv.at[index])
        arrived(xs.at[index], x_recv.at[index])
    wide = xs[...].astype(jnp.float32).reshape(tokens, features)
    factor = factors[...].reshape(tokens, 128)[:, :1]
    normed[...] = (wide * factor * gain[...]).astype(jnp.bfloat16)

    for step in range(chans):
        for part in range(3):
            w_in_copies[step][part].wait()
            terms = contract_last(normed[...], w_in[step, part])
            if step == chans - 1:
                own[part] = terms
                continue
            stage[step, part] = terms.astype(jnp.bfloat16)
            sent.append(send(
                stage.at[step, part], landed.at[chan, part],
                p_send.at[step, part], p_recv.at[chan, part], "chan", chan_others[step],
            ))

    mine = pl.ds(pl.multiple_of(chan * block, block), block)
    featured = []
    for part in range(3):
        value = own[part]
        for index in reversed(chan_others):
            arrived(landed.at[index, part], p_recv.at[index, part])
            value += landed[index, part].astype(jnp.float32)
        featured.append(sum(
            short[lag, part : part + 1, mine] * delayed(value, lag) for lag in range(3)
        ))
    product = featured[1] * featured[2]
    filtered = sum(long_taps[lag : lag + 1] * delayed(product, lag) for lag in range(7))
    gathered[seq] = (featured[0] * filtered).astype(jnp.bfloat16)
    sent += [
        send(gathered.at[seq], gathered.at[seq], g_send.at[step], g_recv.at[seq], "seq", index)
        for step, index in enumerate(seq_others)
    ]

    for step, index in enumerate([seq] + seq_others):
        w_out_copies[step].wait()
        if step > 0:
            arrived(gathered.at[index], g_recv.at[index])
        terms = contract_last(gathered[index], w_out[step])
        if step == 0:
            total[...] = terms
        else:
            total[...] += terms
    leaving[...] = total[...].reshape(leaving.shape).astype(jnp.bfloat16)
    sent += [
        send(leaving.at[index], arriving.at[chan], o_send.at[step], o_recv.at[chan], "chan", index)
        for step, index in enumerate(chan_others)
    ]
    result = total[pl.ds(pl.multiple_of(chan * rows, rows), rows)]
    for index in reversed(chan_others):
        arrived(arriving.at[index], o_recv.at[index])
        result += arriving[index].astype(jnp.float32)
    out_ref[...] = result.astype(jnp.bfloat16)
    for copy in sent:
        copy.wait_send()


def shards(seqs, chans, x_tokens, norm_gain, w_in, short_filter, se_filter, w_out):
    held, features = x_tokens.shape
    columns = w_in.shape[1]
    tokens, block, rows = held * seqs, columns // chans, held * seqs // chans
    weight_bytes = 2 * (w_in.size + w_out.size // chans)
    if (
        seqs < 2 or chans < 2 or held % 8 or rows % 8 or tokens != rows * chans or tokens > 256
        or block * chans != columns or block % 128 or features % 128 or weight_bytes > 40 * MIB
    ):
        return plain(x_tokens, norm_gain, w_in, short_filter, se_filter, w_out)
    bf16, f32 = jnp.bfloat16, jnp.float32
    dma = pltpu.SemaphoreType.DMA
    anywhere = pl.BlockSpec(memory_space=pl.ANY)
    return pl.pallas_call(
        functools.partial(kernel, seqs, chans),
        out_shape=jax.ShapeDtypeStruct((rows, columns), bf16),
        in_specs=[anywhere] * 6,
        out_specs=pl.BlockSpec(memory_space=pltpu.VMEM),
        scratch_shapes=[
            pltpu.VMEM((seqs, held, features), bf16),
            pltpu.VMEM((1, features), f32),
            pltpu.VMEM((chans, 3, block, features), bf16),
            pltpu.VMEM(short_filter.shape, f32),
            pltpu.VMEM(se_filter.shape, f32),
            pltpu.VMEM((seqs, columns, block), bf16),
            pltpu.VMEM((tokens, features), bf16),
            pltpu.VMEM((chans, held, 128), f32),
            pltpu.VMEM((seqs, held, 128), f32),
            pltpu.VMEM((chans - 1, 3, tokens, block), bf16),
            pltpu.VMEM((chans, 3, tokens, block), bf16),
            pltpu.VMEM((3, tokens, block), f32),
            pltpu.VMEM((seqs, tokens, block), bf16),
            pltpu.VMEM((tokens, columns), f32),
            pltpu.VMEM((chans, rows, columns), bf16),
            pltpu.VMEM((chans, rows, columns), bf16),
            dma((4,)), dma((chans, 3)), dma((seqs,)),
            dma((seqs - 1,)), dma((seqs,)),
            dma((chans - 1,)), dma((chans,)),
            dma((seqs - 1,)), dma((seqs,)),
            dma((chans - 1, 3)), dma((chans, 3)),
            dma((seqs - 1,)), dma((seqs,)),
            dma((chans - 1,)), dma((chans,)),
        ],
        compiler_params=pltpu.CompilerParams(
            collective_id=0, has_side_effects=True, vmem_limit_bytes=52 * MIB
        ),
        cost_estimate=pl.CostEstimate(
            flops=tokens * weight_bytes, bytes_accessed=weight_bytes, transcendentals=0
        ),
    )(x_tokens, norm_gain.reshape(1, features), w_in, short_filter, se_filter, w_out)


def solution(mesh):
    placed = (
        P(("parts", "seq"), "chan"),
        P("chan"),
        P(None, "seq", "chan"),
        P(None, None, "seq"),
        P(None, "seq"),
        P("seq", None),
    )
    return jax.shard_map(
        functools.partial(shards, mesh.shape["seq"], mesh.shape["chan"]),
        mesh=mesh, in_specs=placed, out_specs=P(("parts", "chan"), "seq"), check_vma=False,
    )
```

```python
import functools

import jax
import jax.numpy as jnp
from jax import lax
from jax.experimental import pallas as pl
from jax.experimental.pallas import tpu as pltpu
from jax.sharding import PartitionSpec as P

D = 8192
GROUP = 16
MIB = 2**20


epsilon = 1e-06


def from_behind(value, axis, steps):
    count = lax.axis_size(axis)
    leading, last = (max(0, -steps), min(count, count - steps))
    return lax.ppermute(value, axis, [(source, source + steps) for source in range(leading, last)])


def mixer(extended, short_taps, long_taps):
    wide = extended.astype(jnp.float32)
    row_count = wide.shape[0]
    featured = sum(
        (short_taps[offset] * wide[2 - offset : row_count - offset] for offset in range(3))
    )
    queries = featured[:, 0]
    product = featured[:, 1] * featured[:, 2]
    length = product.shape[0]
    filtered = sum(
        (long_taps[offset] * product[6 - offset : length - offset] for offset in range(7))
    )
    return (queries[6:] * filtered).astype(jnp.bfloat16)


def contract_last(left, right):
    return lax.dot_general(
        left, right, (((1,), (1,)), ((), ())), preferred_element_type=jnp.float32
    )


def plain(x_tokens, norm_gain, w_in, short_filter, se_filter, w_out):
    wide = x_tokens.astype(jnp.float32)
    local_squares = jnp.sum(wide * wide, axis=1, keepdims=True)
    total_squares = lax.psum(local_squares, "chan")
    factor = lax.rsqrt(total_squares / D + epsilon)
    normed = (wide * factor * norm_gain).astype(jnp.bfloat16)
    columns = w_in.shape[1]
    flat_in = w_in.reshape(3 * columns, w_in.shape[2])
    piece = lax.all_gather(normed, "seq", axis=0, tiled=True)
    partial_terms = contract_last(piece, flat_in).reshape(piece.shape[0], 3, columns)
    long_full = jnp.repeat(se_filter, GROUP, axis=1)
    mine = lax.psum_scatter(partial_terms, "chan", scatter_dimension=0, tiled=True).astype(
        jnp.bfloat16
    )
    previous = from_behind(mine[-8:], "chan", 1)
    extended = jnp.concatenate([previous, mine], axis=0)
    gated = mixer(extended, short_filter, long_full)
    result = contract_last(lax.all_gather(gated, "seq", axis=1, tiled=True), w_out)
    return result.astype(jnp.bfloat16)


def partners(me, count):
    if count % 2:
        return [lax.rem(me + step, count) for step in range(1, count)]
    chip, core, chips = me // 2, lax.rem(me, 2), count // 2
    found = []
    for step in range(1, chips):
        other = 2 * lax.rem(chip + step, chips)
        found += [other + core, other + 1 - core]
    return found + [2 * chip + 1 - core]


def delayed(value, steps):
    if steps == 0:
        return value
    tokens = lax.broadcasted_iota(jnp.int32, value.shape, 0)
    return jnp.where(tokens >= steps, pltpu.roll(value, steps, 0), 0.0)


def kernel(
    seqs, chans,
    x_hbm, gain_hbm, w_in_hbm, short_hbm, se_hbm, w_out_hbm, out_ref,
    xs, gain, w_in, short, se, w_out, normed, squares, factors, stage, landed, own, gathered, total,
    leaving, arriving,
    small_sem, w_in_sem, w_out_sem, x_send, x_recv, sq_send, sq_recv, f_send, f_recv, p_send, p_recv,
    g_send, g_recv, o_send, o_recv,
):
    seq, chan = lax.axis_index("seq"), lax.axis_index("chan")
    tokens, block = own.shape[1:]
    columns, features = w_out.shape[1], w_in.shape[3]
    rows = out_ref.shape[0]
    seq_others = [lax.rem(seq + step, seqs) for step in range(1, seqs)]
    chan_others = partners(chan, chans)

    def send(source, target, send_sem, recv_sem, axis, index):
        copy = pltpu.make_async_remote_copy(
            src_ref=source, dst_ref=target, send_sem=send_sem, recv_sem=recv_sem,
            device_id={axis: index}, device_id_type=pl.DeviceIdType.MESH,
        )
        copy.start()
        return copy

    def local(source, target, sem):
        copy = pltpu.make_async_copy(source, target, sem)
        copy.start()
        return copy

    def arrived(target, sem):
        pltpu.make_async_copy(target, target, sem).wait()

    x_copy = local(x_hbm, xs.at[seq], small_sem.at[0])
    gain_copy = local(gain_hbm, gain, small_sem.at[1])
    short_copy = local(short_hbm, short, small_sem.at[2])
    se_copy = local(se_hbm, se, small_sem.at[3])
    w_in_copies = []
    for step, index in enumerate(chan_others + [chan]):
        span = pl.ds(pl.multiple_of(index * block, block), block)
        w_in_copies.append([
            local(w_in_hbm.at[part, span], w_in.at[step, part], w_in_sem.at[step, part])
            for part in range(3)
        ])
    w_out_copies = []
    for step, index in enumerate([seq] + seq_others):
        span = pl.ds(pl.multiple_of(index * columns + chan * block, block), block)
        w_out_copies.append(local(w_out_hbm.at[:, span], w_out.at[step], w_out_sem.at[step]))

    barrier = pltpu.get_barrier_semaphore()
    for axis, others in (("seq", seq_others), ("chan", chan_others)):
        for index in others:
            pl.semaphore_signal(
                barrier, inc=1, device_id={axis: index}, device_id_type=pl.DeviceIdType.MESH
            )
    x_copy.wait()
    pl.semaphore_wait(barrier, seqs + chans - 2)

    sent = [
        send(xs.at[seq], xs.at[seq], x_send.at[step], x_recv.at[seq], "seq", index)
        for step, index in enumerate(seq_others)
    ]

    wide = xs[seq].astype(jnp.float32)
    squares[chan] = jnp.broadcast_to(
        jnp.sum(wide * wide, axis=1, keepdims=True), squares.shape[1:]
    )
    sent += [
        send(squares.at[chan], squares.at[chan], sq_send.at[step], sq_recv.at[chan], "chan", index)
        for step, index in enumerate(chan_others)
    ]
    for index in chan_others:
        arrived(squares.at[index], sq_recv.at[index])
    factors[seq] = lax.rsqrt(jnp.sum(squares[...], axis=0) / (features * chans) + epsilon)
    sent += [
        send(factors.at[seq], factors.at[seq], f_send.at[step], f_recv.at[seq], "seq", index)
        for step, index in enumerate(seq_others)
    ]

    se_copy.wait()
    short_copy.wait()
    gain_copy.wait()
    filters = se.shape[1]
    group = columns // filters
    first = lax.broadcasted_iota(jnp.int32, (filters, block), 0) * group
    channel = lax.broadcasted_iota(jnp.int32, (filters, block), 1) + chan * block
    spread = jnp.where((channel >= first) & (channel < first + group), 1.0, 0.0)
    long_taps = jnp.dot(
        se[...], spread, preferred_element_type=jnp.float32, precision=lax.Precision.HIGHEST
    )

    for index in seq_others:
        arrived(factors.at[index], f_recv.at[index])
        arrived(xs.at[index], x_recv.at[index])
    wide = xs[...].astype(jnp.float32).reshape(tokens, features)
    factor = factors[...].reshape(tokens, 128)[:, :1]
    normed[...] = (wide * factor * gain[...]).astype(jnp.bfloat16)

    for step in range(chans):
        for part in range(3):
            w_in_copies[step][part].wait()
            terms = contract_last(w_in[step, part], normed[...]).T
            if step == chans - 1:
                own[part] = terms
                continue
            stage[step, part] = terms.astype(jnp.bfloat16)
            sent.append(send(
                stage.at[step, part], landed.at[chan, part],
                p_send.at[step, part], p_recv.at[chan, part], "chan", chan_others[step],
            ))

    mine = pl.ds(pl.multiple_of(chan * block, block), block)
    featured = []
    for part in range(3):
        value = own[part]
        for index in reversed(chan_others):
            arrived(landed.at[index, part], p_recv.at[index, part])
            value += landed[index, part].astype(jnp.float32)
        featured.append(sum(
            short[lag, part : part + 1, mine] * delayed(value, lag) for lag in range(3)
        ))
    product = featured[1] * featured[2]
    filtered = sum(long_taps[lag : lag + 1] * delayed(product, lag) for lag in range(7))
    gathered[seq] = (featured[0] * filtered).astype(jnp.bfloat16)
    sent += [
        send(gathered.at[seq], gathered.at[seq], g_send.at[step], g_recv.at[seq], "seq", index)
        for step, index in enumerate(seq_others)
    ]

    for step, index in enumerate([seq] + seq_others):
        w_out_copies[step].wait()
        if step > 0:
            arrived(gathered.at[index], g_recv.at[index])
        terms = contract_last(w_out[step], gathered[index]).T
        if step == 0:
            total[...] = terms
        else:
            total[...] += terms
    leaving[...] = total[...].reshape(leaving.shape).astype(jnp.bfloat16)
    sent += [
        send(leaving.at[index], arriving.at[chan], o_send.at[step], o_recv.at[chan], "chan", index)
        for step, index in enumerate(chan_others)
    ]
    result = total[pl.ds(pl.multiple_of(chan * rows, rows), rows)]
    for index in reversed(chan_others):
        arrived(arriving.at[index], o_recv.at[index])
        result += arriving[index].astype(jnp.float32)
    out_ref[...] = result.astype(jnp.bfloat16)
    for copy in sent:
        copy.wait_send()


def shards(seqs, chans, x_tokens, norm_gain, w_in, short_filter, se_filter, w_out):
    held, features = x_tokens.shape
    columns = w_in.shape[1]
    tokens, block, rows = held * seqs, columns // chans, held * seqs // chans
    weight_bytes = 2 * (w_in.size + w_out.size // chans)
    if (
        seqs < 2 or chans < 2 or held % 8 or rows % 8 or tokens != rows * chans or tokens > 256
        or block * chans != columns or block % 128 or features % 128 or weight_bytes > 40 * MIB
    ):
        return plain(x_tokens, norm_gain, w_in, short_filter, se_filter, w_out)
    bf16, f32 = jnp.bfloat16, jnp.float32
    dma = pltpu.SemaphoreType.DMA
    anywhere = pl.BlockSpec(memory_space=pl.ANY)
    return pl.pallas_call(
        functools.partial(kernel, seqs, chans),
        out_shape=jax.ShapeDtypeStruct((rows, columns), bf16),
        in_specs=[anywhere] * 6,
        out_specs=pl.BlockSpec(memory_space=pltpu.VMEM),
        scratch_shapes=[
            pltpu.VMEM((seqs, held, features), bf16),
            pltpu.VMEM((1, features), f32),
            pltpu.VMEM((chans, 3, block, features), bf16),
            pltpu.VMEM(short_filter.shape, f32),
            pltpu.VMEM(se_filter.shape, f32),
            pltpu.VMEM((seqs, columns, block), bf16),
            pltpu.VMEM((tokens, features), bf16),
            pltpu.VMEM((chans, held, 128), f32),
            pltpu.VMEM((seqs, held, 128), f32),
            pltpu.VMEM((chans - 1, 3, tokens, block), bf16),
            pltpu.VMEM((chans, 3, tokens, block), bf16),
            pltpu.VMEM((3, tokens, block), f32),
            pltpu.VMEM((seqs, tokens, block), bf16),
            pltpu.VMEM((tokens, columns), f32),
            pltpu.VMEM((chans, rows, columns), bf16),
            pltpu.VMEM((chans, rows, columns), bf16),
            dma((4,)), dma((chans, 3)), dma((seqs,)),
            dma((seqs - 1,)), dma((seqs,)),
            dma((chans - 1,)), dma((chans,)),
            dma((seqs - 1,)), dma((seqs,)),
            dma((chans - 1, 3)), dma((chans, 3)),
            dma((seqs - 1,)), dma((seqs,)),
            dma((chans - 1,)), dma((chans,)),
        ],
        compiler_params=pltpu.CompilerParams(
            collective_id=0, has_side_effects=True, vmem_limit_bytes=60 * MIB
        ),
        cost_estimate=pl.CostEstimate(
            flops=tokens * weight_bytes, bytes_accessed=weight_bytes, transcendentals=0
        ),
    )(x_tokens, norm_gain.reshape(1, features), w_in, short_filter, se_filter, w_out)


def solution(mesh):
    placed = (
        P(("parts", "seq"), "chan"),
        P("chan"),
        P(None, "seq", "chan"),
        P(None, None, "seq"),
        P(None, "seq"),
        P("seq", None),
    )
    return jax.shard_map(
        functools.partial(shards, mesh.shape["seq"], mesh.shape["chan"]),
        mesh=mesh, in_specs=placed, out_specs=P(("parts", "chan"), "seq"), check_vma=False,
    )
```

```python
import functools

import jax
import jax.numpy as jnp
from jax import lax
from jax.experimental import pallas as pl
from jax.experimental.pallas import tpu as pltpu
from jax.sharding import PartitionSpec as P

D = 8192
GROUP = 16
MIB = 2**20


epsilon = 1e-06


def from_behind(value, axis, steps):
    count = lax.axis_size(axis)
    leading, last = (max(0, -steps), min(count, count - steps))
    return lax.ppermute(value, axis, [(source, source + steps) for source in range(leading, last)])


def mixer(extended, short_taps, long_taps):
    wide = extended.astype(jnp.float32)
    row_count = wide.shape[0]
    featured = sum(
        (short_taps[offset] * wide[2 - offset : row_count - offset] for offset in range(3))
    )
    queries = featured[:, 0]
    product = featured[:, 1] * featured[:, 2]
    length = product.shape[0]
    filtered = sum(
        (long_taps[offset] * product[6 - offset : length - offset] for offset in range(7))
    )
    return (queries[6:] * filtered).astype(jnp.bfloat16)


def contract_last(left, right):
    return lax.dot_general(
        left, right, (((1,), (1,)), ((), ())), preferred_element_type=jnp.float32
    )


def plain(x_tokens, norm_gain, w_in, short_filter, se_filter, w_out):
    wide = x_tokens.astype(jnp.float32)
    local_squares = jnp.sum(wide * wide, axis=1, keepdims=True)
    total_squares = lax.psum(local_squares, "chan")
    factor = lax.rsqrt(total_squares / D + epsilon)
    normed = (wide * factor * norm_gain).astype(jnp.bfloat16)
    columns = w_in.shape[1]
    flat_in = w_in.reshape(3 * columns, w_in.shape[2])
    piece = lax.all_gather(normed, "seq", axis=0, tiled=True)
    partial_terms = contract_last(piece, flat_in).reshape(piece.shape[0], 3, columns)
    long_full = jnp.repeat(se_filter, GROUP, axis=1)
    mine = lax.psum_scatter(partial_terms, "chan", scatter_dimension=0, tiled=True).astype(
        jnp.bfloat16
    )
    previous = from_behind(mine[-8:], "chan", 1)
    extended = jnp.concatenate([previous, mine], axis=0)
    gated = mixer(extended, short_filter, long_full)
    result = contract_last(lax.all_gather(gated, "seq", axis=1, tiled=True), w_out)
    return result.astype(jnp.bfloat16)


def partners(me, count):
    if count % 2:
        return [lax.rem(me + step, count) for step in range(1, count)]
    chip, core, chips = me // 2, lax.rem(me, 2), count // 2
    found = []
    for step in range(1, chips):
        other = 2 * lax.rem(chip + step, chips)
        found += [other + core, other + 1 - core]
    return found + [2 * chip + 1 - core]


def delayed(value, steps):
    if steps == 0:
        return value
    tokens = lax.broadcasted_iota(jnp.int32, value.shape, 0)
    return jnp.where(tokens >= steps, pltpu.roll(value, steps, 0), 0.0)


def kernel(
    seqs, chans,
    x_hbm, gain_hbm, w_in_hbm, short_hbm, se_hbm, w_out_hbm, out_ref,
    xs, gain, w_in, short, se, w_out, normed, squares, factors, stage, landed, own, gathered, total,
    leaving, arriving,
    small_sem, w_in_sem, w_out_sem, x_send, x_recv, sq_send, sq_recv, f_send, f_recv, p_send, p_recv,
    g_send, g_recv, o_send, o_recv,
):
    seq, chan = lax.axis_index("seq"), lax.axis_index("chan")
    tokens, block = own.shape[1:]
    columns, features = w_out.shape[1], w_in.shape[3]
    rows = out_ref.shape[0]
    seq_others = [lax.rem(seq + step, seqs) for step in range(1, seqs)]
    chan_others = partners(chan, chans)

    def send(source, target, send_sem, recv_sem, axis, index):
        copy = pltpu.make_async_remote_copy(
            src_ref=source, dst_ref=target, send_sem=send_sem, recv_sem=recv_sem,
            device_id={axis: index}, device_id_type=pl.DeviceIdType.MESH,
        )
        copy.start()
        return copy

    def local(source, target, sem):
        copy = pltpu.make_async_copy(source, target, sem)
        copy.start()
        return copy

    def arrived(target, sem):
        pltpu.make_async_copy(target, target, sem).wait()

    x_copy = local(x_hbm, xs.at[seq], small_sem.at[0])
    gain_copy = local(gain_hbm, gain, small_sem.at[1])
    short_copy = local(short_hbm, short, small_sem.at[2])
    se_copy = local(se_hbm, se, small_sem.at[3])
    w_in_copies, w_out_copies = [], []

    def fetch_in(step):
        span = pl.ds(pl.multiple_of(in_order[step] * block, block), block)
        w_in_copies.append(local(
            w_in_hbm.at[:, span], w_in.at[step], w_in_sem.at[step]
        ))

    def fetch_out(step):
        span = pl.ds(pl.multiple_of(out_order[step] * columns + chan * block, block), block)
        w_out_copies.append(local(w_out_hbm.at[:, span], w_out.at[step], w_out_sem.at[step]))

    in_order, out_order = chan_others + [chan], [seq] + seq_others
    for step in range(chans // 2):
        fetch_in(step)

    barrier = pltpu.get_barrier_semaphore()
    for axis, others in (("seq", seq_others), ("chan", chan_others)):
        for index in others:
            pl.semaphore_signal(
                barrier, inc=1, device_id={axis: index}, device_id_type=pl.DeviceIdType.MESH
            )
    x_copy.wait()
    pl.semaphore_wait(barrier, seqs + chans - 2)

    sent = [
        send(xs.at[seq], xs.at[seq], x_send.at[step], x_recv.at[seq], "seq", index)
        for step, index in enumerate(seq_others)
    ]

    wide = xs[seq].astype(jnp.float32)
    squares[chan] = jnp.broadcast_to(
        jnp.sum(wide * wide, axis=1, keepdims=True), squares.shape[1:]
    )
    sent += [
        send(squares.at[chan], squares.at[chan], sq_send.at[step], sq_recv.at[chan], "chan", index)
        for step, index in enumerate(chan_others)
    ]
    for index in chan_others:
        arrived(squares.at[index], sq_recv.at[index])
    factors[seq] = lax.rsqrt(jnp.sum(squares[...], axis=0) / (features * chans) + epsilon)
    sent += [
        send(factors.at[seq], factors.at[seq], f_send.at[step], f_recv.at[seq], "seq", index)
        for step, index in enumerate(seq_others)
    ]

    for step in range(len(w_in_copies), chans):
        fetch_in(step)

    se_copy.wait()
    short_copy.wait()
    gain_copy.wait()
    filters = se.shape[1]
    group = columns // filters
    first = lax.broadcasted_iota(jnp.int32, (filters, block), 0) * group
    channel = lax.broadcasted_iota(jnp.int32, (filters, block), 1) + chan * block
    spread = jnp.where((channel >= first) & (channel < first + group), 1.0, 0.0)
    long_taps = jnp.dot(
        se[...], spread, preferred_element_type=jnp.float32, precision=lax.Precision.HIGHEST
    )

    for index in seq_others:
        arrived(factors.at[index], f_recv.at[index])
        arrived(xs.at[index], x_recv.at[index])
    wide = xs[...].astype(jnp.float32).reshape(tokens, features)
    factor = factors[...].reshape(tokens, 128)[:, :1]
    normed[...] = (wide * factor * gain[...]).astype(jnp.bfloat16)

    for step in range(chans):
        w_in_copies[step].wait()
        terms = contract_last(normed[...], w_in[step].reshape(3 * block, features))
        if step < seqs:
            fetch_out(step)
        if step == chans - 1:
            for part in range(3):
                own[part] = terms[:, part * block : (part + 1) * block]
            continue
        for part in range(3):
            stage[step, part] = terms[:, part * block : (part + 1) * block].astype(jnp.bfloat16)
        sent.append(send(
            stage.at[step], landed.at[chan],
            p_send.at[step], p_recv.at[chan], "chan", chan_others[step],
        ))
    for step in range(len(w_out_copies), seqs):
        fetch_out(step)

    mine = pl.ds(pl.multiple_of(chan * block, block), block)
    for index in reversed(chan_others):
        arrived(landed.at[index], p_recv.at[index])
    featured = []
    for part in range(3):
        value = own[part]
        for index in reversed(chan_others):
            value += landed[index, part].astype(jnp.float32)
        featured.append(sum(
            short[lag, part : part + 1, mine] * delayed(value, lag) for lag in range(3)
        ))
    product = featured[1] * featured[2]
    filtered = sum(long_taps[lag : lag + 1] * delayed(product, lag) for lag in range(7))
    gathered[seq] = (featured[0] * filtered).astype(jnp.bfloat16)
    sent += [
        send(gathered.at[seq], gathered.at[seq], g_send.at[step], g_recv.at[seq], "seq", index)
        for step, index in enumerate(seq_others)
    ]

    for step, index in enumerate(out_order):
        w_out_copies[step].wait()
        if step > 0:
            arrived(gathered.at[index], g_recv.at[index])
        terms = contract_last(gathered[index], w_out[step])
        if step == 0:
            total[...] = terms
        else:
            total[...] += terms
    leaving[...] = total[...].reshape(leaving.shape).astype(jnp.bfloat16)
    sent += [
        send(leaving.at[index], arriving.at[chan], o_send.at[step], o_recv.at[chan], "chan", index)
        for step, index in enumerate(chan_others)
    ]
    result = total[pl.ds(pl.multiple_of(chan * rows, rows), rows)]
    for index in reversed(chan_others):
        arrived(arriving.at[index], o_recv.at[index])
        result += arriving[index].astype(jnp.float32)
    out_ref[...] = result.astype(jnp.bfloat16)
    for copy in sent:
        copy.wait_send()


def shards(seqs, chans, x_tokens, norm_gain, w_in, short_filter, se_filter, w_out):
    held, features = x_tokens.shape
    columns = w_in.shape[1]
    tokens, block, rows = held * seqs, columns // chans, held * seqs // chans
    weight_bytes = 2 * (w_in.size + w_out.size // chans)
    if (
        seqs < 2 or chans < 2 or held % 8 or rows % 8 or tokens != rows * chans or tokens > 256
        or block * chans != columns or block % 128 or features % 128 or weight_bytes > 40 * MIB
    ):
        return plain(x_tokens, norm_gain, w_in, short_filter, se_filter, w_out)
    bf16, f32 = jnp.bfloat16, jnp.float32
    dma = pltpu.SemaphoreType.DMA
    anywhere = pl.BlockSpec(memory_space=pl.ANY)
    return pl.pallas_call(
        functools.partial(kernel, seqs, chans),
        out_shape=jax.ShapeDtypeStruct((rows, columns), bf16),
        in_specs=[anywhere] * 6,
        out_specs=pl.BlockSpec(memory_space=pltpu.VMEM),
        scratch_shapes=[
            pltpu.VMEM((seqs, held, features), bf16),
            pltpu.VMEM((1, features), f32),
            pltpu.VMEM((chans, 3, block, features), bf16),
            pltpu.VMEM(short_filter.shape, f32),
            pltpu.VMEM(se_filter.shape, f32),
            pltpu.VMEM((seqs, columns, block), bf16),
            pltpu.VMEM((tokens, features), bf16),
            pltpu.VMEM((chans, held, 128), f32),
            pltpu.VMEM((seqs, held, 128), f32),
            pltpu.VMEM((chans - 1, 3, tokens, block), bf16),
            pltpu.VMEM((chans, 3, tokens, block), bf16),
            pltpu.VMEM((3, tokens, block), f32),
            pltpu.VMEM((seqs, tokens, block), bf16),
            pltpu.VMEM((tokens, columns), f32),
            pltpu.VMEM((chans, rows, columns), bf16),
            pltpu.VMEM((chans, rows, columns), bf16),
            dma((4,)), dma((chans,)), dma((seqs,)),
            dma((seqs - 1,)), dma((seqs,)),
            dma((chans - 1,)), dma((chans,)),
            dma((seqs - 1,)), dma((seqs,)),
            dma((chans - 1,)), dma((chans,)),
            dma((seqs - 1,)), dma((seqs,)),
            dma((chans - 1,)), dma((chans,)),
        ],
        compiler_params=pltpu.CompilerParams(
            collective_id=0, has_side_effects=True, vmem_limit_bytes=60 * MIB
        ),
        cost_estimate=pl.CostEstimate(
            flops=tokens * weight_bytes, bytes_accessed=weight_bytes, transcendentals=0
        ),
    )(x_tokens, norm_gain.reshape(1, features), w_in, short_filter, se_filter, w_out)


def solution(mesh):
    placed = (
        P(("parts", "seq"), "chan"),
        P("chan"),
        P(None, "seq", "chan"),
        P(None, None, "seq"),
        P(None, "seq"),
        P("seq", None),
    )
    return jax.shard_map(
        functools.partial(shards, mesh.shape["seq"], mesh.shape["chan"]),
        mesh=mesh, in_specs=placed, out_specs=P(("parts", "chan"), "seq"), check_vma=False,
    )
```

```python
import functools

import jax
import jax.numpy as jnp
from jax import lax
from jax.experimental import pallas as pl
from jax.experimental.pallas import tpu as pltpu
from jax.sharding import PartitionSpec as P

D = 8192
GROUP = 16
MIB = 2**20


epsilon = 1e-06


def from_behind(value, axis, steps):
    count = lax.axis_size(axis)
    leading, last = (max(0, -steps), min(count, count - steps))
    return lax.ppermute(value, axis, [(source, source + steps) for source in range(leading, last)])


def mixer(extended, short_taps, long_taps):
    wide = extended.astype(jnp.float32)
    row_count = wide.shape[0]
    featured = sum(
        (short_taps[offset] * wide[2 - offset : row_count - offset] for offset in range(3))
    )
    queries = featured[:, 0]
    product = featured[:, 1] * featured[:, 2]
    length = product.shape[0]
    filtered = sum(
        (long_taps[offset] * product[6 - offset : length - offset] for offset in range(7))
    )
    return (queries[6:] * filtered).astype(jnp.bfloat16)


def contract_last(left, right):
    return lax.dot_general(
        left, right, (((1,), (1,)), ((), ())), preferred_element_type=jnp.float32
    )


def plain(x_tokens, norm_gain, w_in, short_filter, se_filter, w_out):
    wide = x_tokens.astype(jnp.float32)
    local_squares = jnp.sum(wide * wide, axis=1, keepdims=True)
    total_squares = lax.psum(local_squares, "chan")
    factor = lax.rsqrt(total_squares / D + epsilon)
    normed = (wide * factor * norm_gain).astype(jnp.bfloat16)
    columns = w_in.shape[1]
    flat_in = w_in.reshape(3 * columns, w_in.shape[2])
    piece = lax.all_gather(normed, "seq", axis=0, tiled=True)
    partial_terms = contract_last(piece, flat_in).reshape(piece.shape[0], 3, columns)
    long_full = jnp.repeat(se_filter, GROUP, axis=1)
    mine = lax.psum_scatter(partial_terms, "chan", scatter_dimension=0, tiled=True).astype(
        jnp.bfloat16
    )
    previous = from_behind(mine[-8:], "chan", 1)
    extended = jnp.concatenate([previous, mine], axis=0)
    gated = mixer(extended, short_filter, long_full)
    result = contract_last(lax.all_gather(gated, "seq", axis=1, tiled=True), w_out)
    return result.astype(jnp.bfloat16)


def partners(me, count):
    if count % 2:
        return [lax.rem(me + step, count) for step in range(1, count)]
    chip, core, chips = me // 2, lax.rem(me, 2), count // 2
    found = []
    for step in range(1, chips):
        other = 2 * lax.rem(chip + step, chips)
        found += [other + core, other + 1 - core]
    return found + [2 * chip + 1 - core]


def delayed(value, steps):
    if steps == 0:
        return value
    tokens = lax.broadcasted_iota(jnp.int32, value.shape, 0)
    return jnp.where(tokens >= steps, pltpu.roll(value, steps, 0), 0.0)


def kernel(
    seqs, chans,
    x_hbm, gain_hbm, w_in_hbm, short_hbm, se_hbm, w_out_hbm, out_ref,
    xs, gain, w_in, short, se, w_out, normed, squares, factors, stage, landed, own, gathered, total,
    leaving, arriving,
    small_sem, w_in_sem, w_out_sem, x_send, x_recv, sq_send, sq_recv, f_send, f_recv, p_send, p_recv,
    g_send, g_recv, o_send, o_recv,
):
    seq, chan = lax.axis_index("seq"), lax.axis_index("chan")
    tokens, block = own.shape[1:]
    columns, features = w_out.shape[1], w_in.shape[3]
    rows = out_ref.shape[0]
    seq_others = [lax.rem(seq + step, seqs) for step in range(1, seqs)]
    chan_others = partners(chan, chans)

    def send(source, target, send_sem, recv_sem, axis, index):
        copy = pltpu.make_async_remote_copy(
            src_ref=source, dst_ref=target, send_sem=send_sem, recv_sem=recv_sem,
            device_id={axis: index}, device_id_type=pl.DeviceIdType.MESH,
        )
        copy.start()
        return copy

    def local(source, target, sem):
        copy = pltpu.make_async_copy(source, target, sem)
        copy.start()
        return copy

    def arrived(target, sem):
        pltpu.make_async_copy(target, target, sem).wait()

    x_copy = local(x_hbm, xs.at[seq], small_sem.at[0])
    gain_copy = local(gain_hbm, gain, small_sem.at[1])
    short_copy = local(short_hbm, short, small_sem.at[2])
    se_copy = local(se_hbm, se, small_sem.at[3])
    w_in_copies, w_out_copies = [], []

    def fetch_in(step):
        span = pl.ds(pl.multiple_of(in_order[step] * block, block), block)
        w_in_copies.append(local(
            w_in_hbm.at[:, span], w_in.at[step], w_in_sem.at[step]
        ))

    def fetch_out(step):
        span = pl.ds(pl.multiple_of(out_order[step] * columns + chan * block, block), block)
        w_out_copies.append(local(w_out_hbm.at[:, span], w_out.at[step], w_out_sem.at[step]))

    in_order, out_order = chan_others + [chan], [seq] + seq_others
    for step in range(chans // 2):
        fetch_in(step)

    barrier = pltpu.get_barrier_semaphore()
    for axis, others in (("seq", seq_others), ("chan", chan_others)):
        for index in others:
            pl.semaphore_signal(
                barrier, inc=1, device_id={axis: index}, device_id_type=pl.DeviceIdType.MESH
            )
    x_copy.wait()
    pl.semaphore_wait(barrier, seqs + chans - 2)

    sent = [
        send(xs.at[seq], xs.at[seq], x_send.at[step], x_recv.at[seq], "seq", index)
        for step, index in enumerate(seq_others)
    ]

    wide = xs[seq].astype(jnp.float32)
    squares[chan] = jnp.broadcast_to(
        jnp.sum(wide * wide, axis=1, keepdims=True), squares.shape[1:]
    )
    sent += [
        send(squares.at[chan], squares.at[chan], sq_send.at[step], sq_recv.at[chan], "chan", index)
        for step, index in enumerate(chan_others)
    ]
    for index in chan_others:
        arrived(squares.at[index], sq_recv.at[index])
    factors[seq] = lax.rsqrt(jnp.sum(squares[...], axis=0) / (features * chans) + epsilon)
    sent += [
        send(factors.at[seq], factors.at[seq], f_send.at[step], f_recv.at[seq], "seq", index)
        for step, index in enumerate(seq_others)
    ]

    for step in range(len(w_in_copies), chans):
        fetch_in(step)

    se_copy.wait()
    short_copy.wait()
    gain_copy.wait()
    filters = se.shape[1]
    group = columns // filters
    first = lax.broadcasted_iota(jnp.int32, (filters, block), 0) * group
    channel = lax.broadcasted_iota(jnp.int32, (filters, block), 1) + chan * block
    spread = jnp.where((channel >= first) & (channel < first + group), 1.0, 0.0)
    long_taps = jnp.dot(
        se[...], spread, preferred_element_type=jnp.float32, precision=lax.Precision.HIGHEST
    )

    for index in seq_others:
        arrived(factors.at[index], f_recv.at[index])
        arrived(xs.at[index], x_recv.at[index])
    wide = xs[...].astype(jnp.float32).reshape(tokens, features)
    factor = factors[...].reshape(tokens, 128)[:, :1]
    normed[...] = (wide * factor * gain[...]).astype(jnp.bfloat16)

    chunk = 256 if block % 256 == 0 else 128
    row = lax.broadcasted_iota(jnp.int32, (tokens, tokens), 0)
    column = lax.broadcasted_iota(jnp.int32, (tokens, tokens), 1)
    identity = jnp.where(row == column, 1.0, 0.0).astype(jnp.bfloat16)
    for step in range(chans):
        w_in_copies[step].wait()
        if step < seqs:
            fetch_out(step)
        for part in range(3):
            for start in range(0, block, chunk):
                terms = contract_last(w_in[step, part, start : start + chunk], normed[...])
                turned = contract_last(identity, terms.astype(jnp.bfloat16))
                if step == chans - 1:
                    own[part, :, start : start + chunk] = turned
                else:
                    stage[step, part, :, start : start + chunk] = turned.astype(jnp.bfloat16)
        if step == chans - 1:
            continue
        sent.append(send(
            stage.at[step], landed.at[chan],
            p_send.at[step], p_recv.at[chan], "chan", chan_others[step],
        ))
    for step in range(len(w_out_copies), seqs):
        fetch_out(step)

    mine = pl.ds(pl.multiple_of(chan * block, block), block)
    for index in reversed(chan_others):
        arrived(landed.at[index], p_recv.at[index])
    featured = []
    for part in range(3):
        value = own[part]
        for index in reversed(chan_others):
            value += landed[index, part].astype(jnp.float32)
        featured.append(sum(
            short[lag, part : part + 1, mine] * delayed(value, lag) for lag in range(3)
        ))
    product = featured[1] * featured[2]
    filtered = sum(long_taps[lag : lag + 1] * delayed(product, lag) for lag in range(7))
    gathered[seq] = (featured[0] * filtered).astype(jnp.bfloat16)
    sent += [
        send(gathered.at[seq], gathered.at[seq], g_send.at[step], g_recv.at[seq], "seq", index)
        for step, index in enumerate(seq_others)
    ]

    for step, index in enumerate(out_order):
        w_out_copies[step].wait()
        if step > 0:
            arrived(gathered.at[index], g_recv.at[index])
        terms = contract_last(gathered[index], w_out[step])
        if step == 0:
            total[...] = terms
        else:
            total[...] += terms
    leaving[...] = total[...].reshape(leaving.shape).astype(jnp.bfloat16)
    sent += [
        send(leaving.at[index], arriving.at[chan], o_send.at[step], o_recv.at[chan], "chan", index)
        for step, index in enumerate(chan_others)
    ]
    result = total[pl.ds(pl.multiple_of(chan * rows, rows), rows)]
    for index in reversed(chan_others):
        arrived(arriving.at[index], o_recv.at[index])
        result += arriving[index].astype(jnp.float32)
    out_ref[...] = result.astype(jnp.bfloat16)
    for copy in sent:
        copy.wait_send()


def shards(seqs, chans, x_tokens, norm_gain, w_in, short_filter, se_filter, w_out):
    held, features = x_tokens.shape
    columns = w_in.shape[1]
    tokens, block, rows = held * seqs, columns // chans, held * seqs // chans
    weight_bytes = 2 * (w_in.size + w_out.size // chans)
    if (
        seqs < 2 or chans < 2 or held % 8 or rows % 8 or tokens != rows * chans or tokens > 256
        or block * chans != columns or block % 128 or features % 128 or weight_bytes > 40 * MIB
    ):
        return plain(x_tokens, norm_gain, w_in, short_filter, se_filter, w_out)
    bf16, f32 = jnp.bfloat16, jnp.float32
    dma = pltpu.SemaphoreType.DMA
    anywhere = pl.BlockSpec(memory_space=pl.ANY)
    return pl.pallas_call(
        functools.partial(kernel, seqs, chans),
        out_shape=jax.ShapeDtypeStruct((rows, columns), bf16),
        in_specs=[anywhere] * 6,
        out_specs=pl.BlockSpec(memory_space=pltpu.VMEM),
        scratch_shapes=[
            pltpu.VMEM((seqs, held, features), bf16),
            pltpu.VMEM((1, features), f32),
            pltpu.VMEM((chans, 3, block, features), bf16),
            pltpu.VMEM(short_filter.shape, f32),
            pltpu.VMEM(se_filter.shape, f32),
            pltpu.VMEM((seqs, columns, block), bf16),
            pltpu.VMEM((tokens, features), bf16),
            pltpu.VMEM((chans, held, 128), f32),
            pltpu.VMEM((seqs, held, 128), f32),
            pltpu.VMEM((chans - 1, 3, tokens, block), bf16),
            pltpu.VMEM((chans, 3, tokens, block), bf16),
            pltpu.VMEM((3, tokens, block), f32),
            pltpu.VMEM((seqs, tokens, block), bf16),
            pltpu.VMEM((tokens, columns), f32),
            pltpu.VMEM((chans, rows, columns), bf16),
            pltpu.VMEM((chans, rows, columns), bf16),
            dma((4,)), dma((chans,)), dma((seqs,)),
            dma((seqs - 1,)), dma((seqs,)),
            dma((chans - 1,)), dma((chans,)),
            dma((seqs - 1,)), dma((seqs,)),
            dma((chans - 1,)), dma((chans,)),
            dma((seqs - 1,)), dma((seqs,)),
            dma((chans - 1,)), dma((chans,)),
        ],
        compiler_params=pltpu.CompilerParams(
            collective_id=0, has_side_effects=True, vmem_limit_bytes=60 * MIB
        ),
        cost_estimate=pl.CostEstimate(
            flops=tokens * weight_bytes, bytes_accessed=weight_bytes, transcendentals=0
        ),
    )(x_tokens, norm_gain.reshape(1, features), w_in, short_filter, se_filter, w_out)


def solution(mesh):
    placed = (
        P(("parts", "seq"), "chan"),
        P("chan"),
        P(None, "seq", "chan"),
        P(None, None, "seq"),
        P(None, "seq"),
        P("seq", None),
    )
    return jax.shard_map(
        functools.partial(shards, mesh.shape["seq"], mesh.shape["chan"]),
        mesh=mesh, in_specs=placed, out_specs=P(("parts", "chan"), "seq"), check_vma=False,
    )
```

```python
import functools

import jax
import jax.numpy as jnp
from jax import lax
from jax.experimental import pallas as pl
from jax.experimental.pallas import tpu as pltpu
from jax.sharding import PartitionSpec as P

D = 8192
GROUP = 16
MIB = 2**20


epsilon = 1e-06


def from_behind(value, axis, steps):
    count = lax.axis_size(axis)
    leading, last = (max(0, -steps), min(count, count - steps))
    return lax.ppermute(value, axis, [(source, source + steps) for source in range(leading, last)])


def mixer(extended, short_taps, long_taps):
    wide = extended.astype(jnp.float32)
    row_count = wide.shape[0]
    featured = sum(
        (short_taps[offset] * wide[2 - offset : row_count - offset] for offset in range(3))
    )
    queries = featured[:, 0]
    product = featured[:, 1] * featured[:, 2]
    length = product.shape[0]
    filtered = sum(
        (long_taps[offset] * product[6 - offset : length - offset] for offset in range(7))
    )
    return (queries[6:] * filtered).astype(jnp.bfloat16)


def contract_last(left, right):
    return lax.dot_general(
        left, right, (((1,), (1,)), ((), ())), preferred_element_type=jnp.float32
    )


def plain(x_tokens, norm_gain, w_in, short_filter, se_filter, w_out):
    wide = x_tokens.astype(jnp.float32)
    local_squares = jnp.sum(wide * wide, axis=1, keepdims=True)
    total_squares = lax.psum(local_squares, "chan")
    factor = lax.rsqrt(total_squares / D + epsilon)
    normed = (wide * factor * norm_gain).astype(jnp.bfloat16)
    columns = w_in.shape[1]
    flat_in = w_in.reshape(3 * columns, w_in.shape[2])
    piece = lax.all_gather(normed, "seq", axis=0, tiled=True)
    partial_terms = contract_last(piece, flat_in).reshape(piece.shape[0], 3, columns)
    long_full = jnp.repeat(se_filter, GROUP, axis=1)
    mine = lax.psum_scatter(partial_terms, "chan", scatter_dimension=0, tiled=True).astype(
        jnp.bfloat16
    )
    previous = from_behind(mine[-8:], "chan", 1)
    extended = jnp.concatenate([previous, mine], axis=0)
    gated = mixer(extended, short_filter, long_full)
    result = contract_last(lax.all_gather(gated, "seq", axis=1, tiled=True), w_out)
    return result.astype(jnp.bfloat16)


def partners(me, count):
    if count % 2:
        return [lax.rem(me + step, count) for step in range(1, count)]
    chip, core, chips = me // 2, lax.rem(me, 2), count // 2
    found = []
    for step in range(1, chips):
        other = 2 * lax.rem(chip + step, chips)
        found += [other + core, other + 1 - core]
    return found + [2 * chip + 1 - core]


def delayed(value, steps):
    if steps == 0:
        return value
    tokens = lax.broadcasted_iota(jnp.int32, value.shape, 0)
    return jnp.where(tokens >= steps, pltpu.roll(value, steps, 0), 0.0)


def kernel(
    parts, seqs, chans,
    x_hbm, gain_hbm, w_in_hbm, short_hbm, se_hbm, w_out_hbm, out_ref,
    xs, gain, w_in, short, se, w_out, normed, squares, factors, stage, landed, own, gathered, total,
    leaving, arriving,
    small_sem, w_in_sem, w_out_sem, x_send, xp_send, x_recv, sq_send, sq_recv, f_send, f_recv,
    fp_send, fp_recv, p_send, p_recv, g_send, g_recv, o_send, o_recv,
):
    part, seq, chan = lax.axis_index("parts"), lax.axis_index("seq"), lax.axis_index("chan")
    tokens, features = normed.shape[1:]
    columns, block = w_out.shape[1:]
    rows = out_ref.shape[0]
    part_others = [lax.rem(part + step, parts) for step in range(1, parts)]
    seq_others = [lax.rem(seq + step, seqs) for step in range(1, seqs)]
    chan_others = partners(chan, chans)
    plane = [(one, other) for one in part_others for other in chan_others + [chan]]
    plane += [(part, other) for other in chan_others]

    def send(source, target, send_sem, recv_sem, **device):
        copy = pltpu.make_async_remote_copy(
            src_ref=source, dst_ref=target, send_sem=send_sem, recv_sem=recv_sem,
            device_id=device, device_id_type=pl.DeviceIdType.MESH,
        )
        copy.start()
        sent.append(copy)

    def local(source, target, sem):
        copy = pltpu.make_async_copy(source, target, sem)
        copy.start()
        return copy

    def arrived(target, sem):
        pltpu.make_async_copy(target, target, sem).wait()

    def mine(index):
        return pl.multiple_of((index * parts + part) * block, block)

    sent = []
    x_copy = local(x_hbm, xs.at[part, seq], small_sem.at[0])
    gain_copy = local(gain_hbm, gain, small_sem.at[1])
    short_copy = local(short_hbm, short, small_sem.at[2])
    se_copy = local(se_hbm, se, small_sem.at[3])
    w_in_copies = [
        local(w_in_hbm.at[:, pl.ds(mine(index), block)], w_in.at[step], w_in_sem.at[step])
        for step, index in enumerate(chan_others + [chan])
    ]

    barrier = pltpu.get_barrier_semaphore()
    greeted = [{"seq": index} for index in seq_others]
    greeted += [{"parts": one, "chan": other} for one, other in plane]
    for device in greeted:
        pl.semaphore_signal(
            barrier, inc=1, device_id=device, device_id_type=pl.DeviceIdType.MESH
        )
    x_copy.wait()
    pl.semaphore_wait(barrier, len(greeted))

    for step, index in enumerate(seq_others):
        slab = xs.at[part, seq]
        send(slab, slab, x_send.at[step], x_recv.at[part, seq], seq=index)

    def relay(step, index):
        slab = xs.at[part, index]
        for hop, other in enumerate(part_others):
            send(slab, slab, xp_send.at[hop, step], x_recv.at[part, index], parts=other)

    relay(0, seq)

    wide = xs[part, seq].astype(jnp.float32)
    squares[chan] = jnp.broadcast_to(
        jnp.sum(wide * wide, axis=1, keepdims=True), squares.shape[1:]
    )
    for step, index in enumerate(chan_others):
        slab = squares.at[chan]
        send(slab, slab, sq_send.at[step], sq_recv.at[chan], chan=index)
    w_out_copies = [
        local(
            w_out_hbm.at[:, pl.ds(pl.multiple_of(index * columns + mine(chan), block), block)],
            w_out.at[step], w_out_sem.at[step],
        )
        for step, index in enumerate([seq] + seq_others)
    ]
    for index in chan_others:
        arrived(squares.at[index], sq_recv.at[index])
    factors[part, seq] = lax.rsqrt(jnp.sum(squares[...], axis=0) / (features * chans) + epsilon)
    for step, index in enumerate(seq_others):
        slab = factors.at[part, seq]
        send(slab, slab, f_send.at[step], f_recv.at[seq], seq=index)

    se_copy.wait()
    short_copy.wait()
    gain_copy.wait()
    filters = se.shape[1]
    group = columns // filters
    first = lax.broadcasted_iota(jnp.int32, (filters, block), 0) * group
    channel = lax.broadcasted_iota(jnp.int32, (filters, block), 1) + mine(chan)
    spread = jnp.where((channel >= first) & (channel < first + group), 1.0, 0.0)
    long_taps = jnp.dot(
        se[...], spread, preferred_element_type=jnp.float32, precision=lax.Precision.HIGHEST
    )

    for step, index in enumerate(seq_others):
        arrived(xs.at[part, index], x_recv.at[part, index])
        relay(step + 1, index)
    for index in seq_others:
        arrived(factors.at[part, index], f_recv.at[index])
    for hop, other in enumerate(part_others):
        slab = factors.at[part]
        send(slab, slab, fp_send.at[hop], fp_recv.at[part], parts=other)

    def normalize(one):
        wide = xs[one].astype(jnp.float32).reshape(tokens, features)
        factor = factors[one].reshape(tokens, 128)[:, :1]
        normed[one] = (wide * factor * gain[...]).astype(jnp.bfloat16)

    normalize(part)
    for other in part_others:
        arrived(factors.at[other], fp_recv.at[other])
        for index in [seq] + seq_others:
            arrived(xs.at[other, index], x_recv.at[other, index])
        normalize(other)

    for step in range(chans):
        w_in_copies[step].wait()
        terms = contract_last(
            normed[...].reshape(parts * tokens, features), w_in[step].reshape(3 * block, features)
        )
        for kind in range(3):
            piece = terms[:, kind * block : (kind + 1) * block]
            if step == chans - 1:
                own[kind] = piece
            else:
                stage[step, kind] = piece.astype(jnp.bfloat16)
        if step < chans - 1:
            send(
                stage.at[step], landed.at[chan],
                p_send.at[step], p_recv.at[chan], chan=chan_others[step],
            )

    for index in reversed(chan_others):
        arrived(landed.at[index], p_recv.at[index])
    for one in range(parts):
        window = slice(one * tokens, (one + 1) * tokens)
        featured = []
        for kind in range(3):
            value = own[kind, window]
            for index in reversed(chan_others):
                value += landed[index, kind, window].astype(jnp.float32)
            featured.append(sum(
                short[lag, kind : kind + 1, pl.ds(mine(chan), block)] * delayed(value, lag)
                for lag in range(3)
            ))
        product = featured[1] * featured[2]
        filtered = sum(long_taps[lag : lag + 1] * delayed(product, lag) for lag in range(7))
        gathered[seq, window] = (featured[0] * filtered).astype(jnp.bfloat16)
    for step, index in enumerate(seq_others):
        slab = gathered.at[seq]
        send(slab, slab, g_send.at[step], g_recv.at[seq], seq=index)

    for step, index in enumerate([seq] + seq_others):
        w_out_copies[step].wait()
        if step > 0:
            arrived(gathered.at[index], g_recv.at[index])
        terms = contract_last(gathered[index], w_out[step])
        if step == 0:
            total[...] = terms
        else:
            total[...] += terms
    leaving[...] = total[...].reshape(leaving.shape).astype(jnp.bfloat16)
    for step, (one, other) in enumerate(plane):
        send(
            leaving.at[one, other], arriving.at[part, chan],
            o_send.at[step], o_recv.at[part, chan], parts=one, chan=other,
        )
    result = total[pl.ds(pl.multiple_of((part * chans + chan) * rows, rows), rows)]
    for one, other in reversed(plane):
        arrived(arriving.at[one, other], o_recv.at[one, other])
        result += arriving[one, other].astype(jnp.float32)
    out_ref[...] = result.astype(jnp.bfloat16)
    for copy in sent:
        copy.wait_send()


def shards(parts, seqs, chans, x_tokens, norm_gain, w_in, short_filter, se_filter, w_out):
    held, features = x_tokens.shape
    columns = w_in.shape[1]
    tokens, block, rows = held * seqs, columns // (chans * parts), held * seqs // chans
    weight_bytes = 2 * (w_in.size + w_out.size // chans) // parts
    if (
        seqs < 2 or chans < 2 or held % 8 or rows % 8 or tokens % 16 or tokens != rows * chans
        or tokens * parts > 128 or block * chans * parts != columns or block % 128
        or features % 128 or weight_bytes > 32 * MIB
    ):
        return plain(x_tokens, norm_gain, w_in, short_filter, se_filter, w_out)
    bf16, f32 = jnp.bfloat16, jnp.float32
    dma = pltpu.SemaphoreType.DMA
    anywhere = pl.BlockSpec(memory_space=pl.ANY)
    every = parts * tokens
    return pl.pallas_call(
        functools.partial(kernel, parts, seqs, chans),
        out_shape=jax.ShapeDtypeStruct((rows, columns), bf16),
        in_specs=[anywhere] * 6,
        out_specs=pl.BlockSpec(memory_space=pltpu.VMEM),
        scratch_shapes=[
            pltpu.VMEM((parts, seqs, held, features), bf16),
            pltpu.VMEM((1, features), f32),
            pltpu.VMEM((chans, 3, block, features), bf16),
            pltpu.VMEM(short_filter.shape, f32),
            pltpu.VMEM(se_filter.shape, f32),
            pltpu.VMEM((seqs, columns, block), bf16),
            pltpu.VMEM((parts, tokens, features), bf16),
            pltpu.VMEM((chans, held, 128), f32),
            pltpu.VMEM((parts, seqs, held, 128), f32),
            pltpu.VMEM((chans - 1, 3, every, block), bf16),
            pltpu.VMEM((chans, 3, every, block), bf16),
            pltpu.VMEM((3, every, block), f32),
            pltpu.VMEM((seqs, every, block), bf16),
            pltpu.VMEM((every, columns), f32),
            pltpu.VMEM((parts, chans, rows, columns), bf16),
            pltpu.VMEM((parts, chans, rows, columns), bf16),
            dma((4,)), dma((chans,)), dma((seqs,)),
            dma((seqs - 1,)), dma((max(parts - 1, 1), seqs)), dma((parts, seqs)),
            dma((chans - 1,)), dma((chans,)),
            dma((seqs - 1,)), dma((seqs,)),
            dma((max(parts - 1, 1),)), dma((parts,)),
            dma((chans - 1,)), dma((chans,)),
            dma((seqs - 1,)), dma((seqs,)),
            dma((parts * chans - 1,)), dma((parts, chans)),
        ],
        compiler_params=pltpu.CompilerParams(
            collective_id=0, has_side_effects=True, vmem_limit_bytes=60 * MIB
        ),
        cost_estimate=pl.CostEstimate(
            flops=every * weight_bytes, bytes_accessed=weight_bytes, transcendentals=0
        ),
    )(x_tokens, norm_gain.reshape(1, features), w_in, short_filter, se_filter, w_out)


def solution(mesh):
    placed = (
        P(("parts", "seq"), "chan"),
        P("chan"),
        P(None, "seq", "chan"),
        P(None, None, "seq"),
        P(None, "seq"),
        P("seq", None),
    )
    return jax.shard_map(
        functools.partial(shards, *(mesh.shape[axis] for axis in ("parts", "seq", "chan"))),
        mesh=mesh, in_specs=placed, out_specs=P(("parts", "chan"), "seq"), check_vma=False,
    )
```

```python
import functools

import jax
import jax.numpy as jnp
from jax import lax
from jax.experimental import pallas as pl
from jax.experimental.pallas import tpu as pltpu
from jax.sharding import PartitionSpec as P

D = 8192
GROUP = 16
MIB = 2**20


epsilon = 1e-06


def from_behind(value, axis, steps):
    count = lax.axis_size(axis)
    leading, last = (max(0, -steps), min(count, count - steps))
    return lax.ppermute(value, axis, [(source, source + steps) for source in range(leading, last)])


def mixer(extended, short_taps, long_taps):
    wide = extended.astype(jnp.float32)
    row_count = wide.shape[0]
    featured = sum(
        (short_taps[offset] * wide[2 - offset : row_count - offset] for offset in range(3))
    )
    queries = featured[:, 0]
    product = featured[:, 1] * featured[:, 2]
    length = product.shape[0]
    filtered = sum(
        (long_taps[offset] * product[6 - offset : length - offset] for offset in range(7))
    )
    return (queries[6:] * filtered).astype(jnp.bfloat16)


def contract_last(left, right):
    return lax.dot_general(
        left, right, (((1,), (1,)), ((), ())), preferred_element_type=jnp.float32
    )


def plain(x_tokens, norm_gain, w_in, short_filter, se_filter, w_out):
    wide = x_tokens.astype(jnp.float32)
    local_squares = jnp.sum(wide * wide, axis=1, keepdims=True)
    total_squares = lax.psum(local_squares, "chan")
    factor = lax.rsqrt(total_squares / D + epsilon)
    normed = (wide * factor * norm_gain).astype(jnp.bfloat16)
    columns = w_in.shape[1]
    flat_in = w_in.reshape(3 * columns, w_in.shape[2])
    piece = lax.all_gather(normed, "seq", axis=0, tiled=True)
    partial_terms = contract_last(piece, flat_in).reshape(piece.shape[0], 3, columns)
    long_full = jnp.repeat(se_filter, GROUP, axis=1)
    mine = lax.psum_scatter(partial_terms, "chan", scatter_dimension=0, tiled=True).astype(
        jnp.bfloat16
    )
    previous = from_behind(mine[-8:], "chan", 1)
    extended = jnp.concatenate([previous, mine], axis=0)
    gated = mixer(extended, short_filter, long_full)
    result = contract_last(lax.all_gather(gated, "seq", axis=1, tiled=True), w_out)
    return result.astype(jnp.bfloat16)


def partners(me, count):
    if count % 2:
        return [lax.rem(me + step, count) for step in range(1, count)]
    chip, core, chips = me // 2, lax.rem(me, 2), count // 2
    found = []
    for step in range(1, chips):
        other = 2 * lax.rem(chip + step, chips)
        found += [other + core, other + 1 - core]
    return found + [2 * chip + 1 - core]


def delayed(value, steps):
    if steps == 0:
        return value
    tokens = lax.broadcasted_iota(jnp.int32, value.shape, 0)
    return jnp.where(tokens >= steps, pltpu.roll(value, steps, 0), 0.0)


def kernel(
    seqs, chans,
    x_hbm, gain_hbm, w_in_hbm, short_hbm, se_hbm, w_out_hbm, out_ref,
    xs, gain, w_in, short, se, w_out, normed, squares, factors, stage, landed, own, gathered, total,
    leaving, arriving,
    small_sem, w_in_sem, w_out_sem, x_send, x_recv, sq_send, sq_recv, f_send, f_recv, p_send, p_recv,
    g_send, g_recv, o_send, o_recv,
):
    seq, chan = lax.axis_index("seq"), lax.axis_index("chan")
    halves, tokens, part = own.shape[0], own.shape[2], own.shape[3]
    block = halves * part
    columns, features = w_out.shape[1], w_in.shape[4]
    rows = out_ref.shape[0]
    seq_others = [lax.rem(seq + step, seqs) for step in range(1, seqs)]
    chan_others = partners(chan, chans)

    def send(source, target, send_sem, recv_sem, axis, index):
        copy = pltpu.make_async_remote_copy(
            src_ref=source, dst_ref=target, send_sem=send_sem, recv_sem=recv_sem,
            device_id={axis: index}, device_id_type=pl.DeviceIdType.MESH,
        )
        copy.start()
        return copy

    def local(source, target, sem):
        copy = pltpu.make_async_copy(source, target, sem)
        copy.start()
        return copy

    def arrived(target, sem):
        pltpu.make_async_copy(target, target, sem).wait()

    x_copy = local(x_hbm, xs.at[seq], small_sem.at[0])
    gain_copy = local(gain_hbm, gain, small_sem.at[1])
    short_copy = local(short_hbm, short, small_sem.at[2])
    se_copy = local(se_hbm, se, small_sem.at[3])
    in_order, out_order = chan_others + [chan], [seq] + seq_others

    def fetch_in(half, step):
        span = pl.ds(pl.multiple_of(in_order[step] * block + half * part, part), part)
        return local(w_in_hbm.at[:, span], w_in.at[half, step], w_in_sem.at[half, step])

    def fetch_out(step):
        span = pl.ds(pl.multiple_of(out_order[step] * columns + chan * block, block), block)
        return local(w_out_hbm.at[:, span], w_out.at[step], w_out_sem.at[step])

    w_in_copies = [[fetch_in(0, step) for step in range(chans)]]

    barrier = pltpu.get_barrier_semaphore()
    for axis, others in (("seq", seq_others), ("chan", chan_others)):
        for index in others:
            pl.semaphore_signal(
                barrier, inc=1, device_id={axis: index}, device_id_type=pl.DeviceIdType.MESH
            )
    x_copy.wait()
    pl.semaphore_wait(barrier, seqs + chans - 2)

    sent = [
        send(xs.at[seq], xs.at[seq], x_send.at[step], x_recv.at[seq], "seq", index)
        for step, index in enumerate(seq_others)
    ]

    wide = xs[seq].astype(jnp.float32)
    squares[chan] = jnp.broadcast_to(
        jnp.sum(wide * wide, axis=1, keepdims=True), squares.shape[1:]
    )
    sent += [
        send(squares.at[chan], squares.at[chan], sq_send.at[step], sq_recv.at[chan], "chan", index)
        for step, index in enumerate(chan_others)
    ]
    for index in chan_others:
        arrived(squares.at[index], sq_recv.at[index])
    factors[seq] = lax.rsqrt(jnp.sum(squares[...], axis=0) / (features * chans) + epsilon)
    sent += [
        send(factors.at[seq], factors.at[seq], f_send.at[step], f_recv.at[seq], "seq", index)
        for step, index in enumerate(seq_others)
    ]

    for half in range(1, halves):
        w_in_copies.append([fetch_in(half, step) for step in range(chans)])
    w_out_copies = [fetch_out(step) for step in range(seqs)]

    se_copy.wait()
    short_copy.wait()
    gain_copy.wait()
    filters = se.shape[1]
    group = columns // filters
    first = lax.broadcasted_iota(jnp.int32, (filters, block), 0) * group
    channel = lax.broadcasted_iota(jnp.int32, (filters, block), 1) + chan * block
    spread = jnp.where((channel >= first) & (channel < first + group), 1.0, 0.0)
    long_taps = jnp.dot(
        se[...], spread, preferred_element_type=jnp.float32, precision=lax.Precision.HIGHEST
    )

    for index in seq_others:
        arrived(factors.at[index], f_recv.at[index])
        arrived(xs.at[index], x_recv.at[index])
    wide = xs[...].astype(jnp.float32).reshape(tokens, features)
    factor = factors[...].reshape(tokens, 128)[:, :1]
    normed[...] = (wide * factor * gain[...]).astype(jnp.bfloat16)

    def mix(half):
        for index in reversed(chan_others):
            arrived(landed.at[half, index], p_recv.at[half, index])
        start = half * part
        mine = pl.ds(pl.multiple_of(chan * block + start, part), part)
        taps = long_taps[:, start : start + part]
        featured = []
        for kind in range(3):
            value = own[half, kind]
            for index in reversed(chan_others):
                value += landed[half, index, kind].astype(jnp.float32)
            featured.append(sum(
                short[lag, kind : kind + 1, mine] * delayed(value, lag) for lag in range(3)
            ))
        product = featured[1] * featured[2]
        filtered = sum(taps[lag : lag + 1] * delayed(product, lag) for lag in range(7))
        gathered[half, seq] = (featured[0] * filtered).astype(jnp.bfloat16)
        slab = gathered.at[half, seq]
        sent.extend([
            send(slab, slab, g_send.at[half, step], g_recv.at[half, seq], "seq", index)
            for step, index in enumerate(seq_others)
        ])

    for half in range(halves):
        for step in range(chans):
            w_in_copies[half][step].wait()
            terms = contract_last(normed[...], w_in[half, step].reshape(3 * part, features))
            for kind in range(3):
                piece = terms[:, kind * part : (kind + 1) * part]
                if step == chans - 1:
                    own[half, kind] = piece
                else:
                    stage[half, step, kind] = piece.astype(jnp.bfloat16)
            if step < chans - 1:
                sent.append(send(
                    stage.at[half, step], landed.at[half, chan],
                    p_send.at[half, step], p_recv.at[half, chan], "chan", chan_others[step],
                ))
            if half > 0 and step == min(1, chans - 2):
                mix(half - 1)
    mix(halves - 1)

    for half in range(halves):
        for step, index in enumerate(out_order):
            if half == 0:
                w_out_copies[step].wait()
            if step > 0:
                arrived(gathered.at[half, index], g_recv.at[half, index])
            terms = contract_last(
                gathered[half, index], w_out[step, :, half * part : (half + 1) * part]
            )
            if half == 0 and step == 0:
                total[...] = terms
            else:
                total[...] += terms
    leaving[...] = total[...].reshape(leaving.shape).astype(jnp.bfloat16)
    sent += [
        send(leaving.at[index], arriving.at[chan], o_send.at[step], o_recv.at[chan], "chan", index)
        for step, index in enumerate(chan_others)
    ]
    result = total[pl.ds(pl.multiple_of(chan * rows, rows), rows)]
    for index in reversed(chan_others):
        arrived(arriving.at[index], o_recv.at[index])
        result += arriving[index].astype(jnp.float32)
    out_ref[...] = result.astype(jnp.bfloat16)
    for copy in sent:
        copy.wait_send()


def shards(seqs, chans, x_tokens, norm_gain, w_in, short_filter, se_filter, w_out):
    held, features = x_tokens.shape
    columns = w_in.shape[1]
    tokens, block, rows = held * seqs, columns // chans, held * seqs // chans
    halves = 2 if block % 256 == 0 else 1
    part = block // halves
    weight_bytes = 2 * (w_in.size + w_out.size // chans)
    if (
        seqs < 2 or chans < 2 or held % 8 or rows % 8 or tokens != rows * chans or tokens > 256
        or block * chans != columns or block % 128 or features % 128 or weight_bytes > 40 * MIB
    ):
        return plain(x_tokens, norm_gain, w_in, short_filter, se_filter, w_out)
    bf16, f32 = jnp.bfloat16, jnp.float32
    dma = pltpu.SemaphoreType.DMA
    anywhere = pl.BlockSpec(memory_space=pl.ANY)
    return pl.pallas_call(
        functools.partial(kernel, seqs, chans),
        out_shape=jax.ShapeDtypeStruct((rows, columns), bf16),
        in_specs=[anywhere] * 6,
        out_specs=pl.BlockSpec(memory_space=pltpu.VMEM),
        scratch_shapes=[
            pltpu.VMEM((seqs, held, features), bf16),
            pltpu.VMEM((1, features), f32),
            pltpu.VMEM((halves, chans, 3, part, features), bf16),
            pltpu.VMEM(short_filter.shape, f32),
            pltpu.VMEM(se_filter.shape, f32),
            pltpu.VMEM((seqs, columns, block), bf16),
            pltpu.VMEM((tokens, features), bf16),
            pltpu.VMEM((chans, held, 128), f32),
            pltpu.VMEM((seqs, held, 128), f32),
            pltpu.VMEM((halves, chans - 1, 3, tokens, part), bf16),
            pltpu.VMEM((halves, chans, 3, tokens, part), bf16),
            pltpu.VMEM((halves, 3, tokens, part), f32),
            pltpu.VMEM((halves, seqs, tokens, part), bf16),
            pltpu.VMEM((tokens, columns), f32),
            pltpu.VMEM((chans, rows, columns), bf16),
            pltpu.VMEM((chans, rows, columns), bf16),
            dma((4,)), dma((halves, chans)), dma((seqs,)),
            dma((seqs - 1,)), dma((seqs,)),
            dma((chans - 1,)), dma((chans,)),
            dma((seqs - 1,)), dma((seqs,)),
            dma((halves, chans - 1)), dma((halves, chans)),
            dma((halves, seqs - 1)), dma((halves, seqs)),
            dma((chans - 1,)), dma((chans,)),
        ],
        compiler_params=pltpu.CompilerParams(
            collective_id=0, has_side_effects=True, vmem_limit_bytes=60 * MIB
        ),
        cost_estimate=pl.CostEstimate(
            flops=tokens * weight_bytes, bytes_accessed=weight_bytes, transcendentals=0
        ),
    )(x_tokens, norm_gain.reshape(1, features), w_in, short_filter, se_filter, w_out)


def solution(mesh):
    placed = (
        P(("parts", "seq"), "chan"),
        P("chan"),
        P(None, "seq", "chan"),
        P(None, None, "seq"),
        P(None, "seq"),
        P("seq", None),
    )
    return jax.shard_map(
        functools.partial(shards, mesh.shape["seq"], mesh.shape["chan"]),
        mesh=mesh, in_specs=placed, out_specs=P(("parts", "chan"), "seq"), check_vma=False,
    )
```

```python
import functools

import jax
import jax.numpy as jnp
from jax import lax
from jax.experimental import pallas as pl
from jax.experimental.pallas import tpu as pltpu
from jax.sharding import PartitionSpec as P

D = 8192
GROUP = 16
MIB = 2**20


epsilon = 1e-06


def from_behind(value, axis, steps):
    count = lax.axis_size(axis)
    leading, last = (max(0, -steps), min(count, count - steps))
    return lax.ppermute(value, axis, [(source, source + steps) for source in range(leading, last)])


def mixer(extended, short_taps, long_taps):
    wide = extended.astype(jnp.float32)
    row_count = wide.shape[0]
    featured = sum(
        (short_taps[offset] * wide[2 - offset : row_count - offset] for offset in range(3))
    )
    queries = featured[:, 0]
    product = featured[:, 1] * featured[:, 2]
    length = product.shape[0]
    filtered = sum(
        (long_taps[offset] * product[6 - offset : length - offset] for offset in range(7))
    )
    return (queries[6:] * filtered).astype(jnp.bfloat16)


def contract_last(left, right):
    return lax.dot_general(
        left, right, (((1,), (1,)), ((), ())), preferred_element_type=jnp.float32
    )


def plain(x_tokens, norm_gain, w_in, short_filter, se_filter, w_out):
    wide = x_tokens.astype(jnp.float32)
    local_squares = jnp.sum(wide * wide, axis=1, keepdims=True)
    total_squares = lax.psum(local_squares, "chan")
    factor = lax.rsqrt(total_squares / D + epsilon)
    normed = (wide * factor * norm_gain).astype(jnp.bfloat16)
    columns = w_in.shape[1]
    flat_in = w_in.reshape(3 * columns, w_in.shape[2])
    piece = lax.all_gather(normed, "seq", axis=0, tiled=True)
    partial_terms = contract_last(piece, flat_in).reshape(piece.shape[0], 3, columns)
    long_full = jnp.repeat(se_filter, GROUP, axis=1)
    mine = lax.psum_scatter(partial_terms, "chan", scatter_dimension=0, tiled=True).astype(
        jnp.bfloat16
    )
    previous = from_behind(mine[-8:], "chan", 1)
    extended = jnp.concatenate([previous, mine], axis=0)
    gated = mixer(extended, short_filter, long_full)
    result = contract_last(lax.all_gather(gated, "seq", axis=1, tiled=True), w_out)
    return result.astype(jnp.bfloat16)


def partners(me, count):
    if count % 2:
        return [lax.rem(me + step, count) for step in range(1, count)]
    chip, core, chips = me // 2, lax.rem(me, 2), count // 2
    found = []
    for step in range(1, chips):
        other = 2 * lax.rem(chip + step, chips)
        found += [other + core, other + 1 - core]
    return found + [2 * chip + 1 - core]


def nearest_first(me, count):
    found = partners(me, count)
    return found if count % 2 else found[-1:] + found[:-1]


def delayed(value, steps):
    if steps == 0:
        return value
    tokens = lax.broadcasted_iota(jnp.int32, value.shape, 0)
    return jnp.where(tokens >= steps, pltpu.roll(value, steps, 0), 0.0)


def kernel(
    seqs, chans,
    x_hbm, gain_hbm, w_in_hbm, short_hbm, se_hbm, w_out_hbm, out_ref,
    xs, gain, w_in, short, se, w_out, normed, squares, factors, stage, landed, own, gathered, total,
    leaving, arriving,
    small_sem, w_in_sem, w_out_sem, x_send, x_recv, sq_send, sq_recv, f_send, f_recv, p_send, p_recv,
    g_send, g_recv, o_send, o_recv,
):
    seq, chan = lax.axis_index("seq"), lax.axis_index("chan")
    tokens, block = own.shape[1:]
    columns, features = w_out.shape[1], w_in.shape[3]
    rows = out_ref.shape[0]
    seq_others = nearest_first(seq, seqs)
    chan_others = partners(chan, chans)

    def send(source, target, send_sem, recv_sem, axis, index):
        copy = pltpu.make_async_remote_copy(
            src_ref=source, dst_ref=target, send_sem=send_sem, recv_sem=recv_sem,
            device_id={axis: index}, device_id_type=pl.DeviceIdType.MESH,
        )
        copy.start()
        return copy

    def local(source, target, sem):
        copy = pltpu.make_async_copy(source, target, sem)
        copy.start()
        return copy

    def arrived(target, sem):
        pltpu.make_async_copy(target, target, sem).wait()

    x_copy = local(x_hbm, xs.at[seq], small_sem.at[0])
    gain_copy = local(gain_hbm, gain, small_sem.at[1])
    short_copy = local(short_hbm, short, small_sem.at[2])
    se_copy = local(se_hbm, se, small_sem.at[3])
    w_in_copies, w_out_copies = [], []

    def fetch_in(step):
        span = pl.ds(pl.multiple_of(in_order[step] * block, block), block)
        w_in_copies.append(local(
            w_in_hbm.at[:, span], w_in.at[step], w_in_sem.at[step]
        ))

    def fetch_out(step):
        span = pl.ds(pl.multiple_of(out_order[step] * columns + chan * block, block), block)
        w_out_copies.append(local(w_out_hbm.at[:, span], w_out.at[step], w_out_sem.at[step]))

    in_order, out_order = chan_others + [chan], [seq] + seq_others
    for step in range(chans // 2):
        fetch_in(step)

    barrier = pltpu.get_barrier_semaphore()
    for axis, others in (("seq", seq_others), ("chan", chan_others)):
        for index in others:
            pl.semaphore_signal(
                barrier, inc=1, device_id={axis: index}, device_id_type=pl.DeviceIdType.MESH
            )
    x_copy.wait()
    pl.semaphore_wait(barrier, seqs + chans - 2)

    sent = [
        send(xs.at[seq], xs.at[seq], x_send.at[step], x_recv.at[seq], "seq", index)
        for step, index in reversed(list(enumerate(seq_others)))
    ]

    wide = xs[seq].astype(jnp.float32)
    squares[chan] = jnp.broadcast_to(
        jnp.sum(wide * wide, axis=1, keepdims=True), squares.shape[1:]
    )
    sent += [
        send(squares.at[chan], squares.at[chan], sq_send.at[step], sq_recv.at[chan], "chan", index)
        for step, index in enumerate(chan_others)
    ]
    for index in chan_others:
        arrived(squares.at[index], sq_recv.at[index])
    factors[seq] = lax.rsqrt(jnp.sum(squares[...], axis=0) / (features * chans) + epsilon)
    sent += [
        send(factors.at[seq], factors.at[seq], f_send.at[step], f_recv.at[seq], "seq", index)
        for step, index in reversed(list(enumerate(seq_others)))
    ]

    for step in range(len(w_in_copies), chans):
        fetch_in(step)

    se_copy.wait()
    short_copy.wait()
    gain_copy.wait()
    filters = se.shape[1]
    group = columns // filters
    first = lax.broadcasted_iota(jnp.int32, (filters, block), 0) * group
    channel = lax.broadcasted_iota(jnp.int32, (filters, block), 1) + chan * block
    spread = jnp.where((channel >= first) & (channel < first + group), 1.0, 0.0)
    long_taps = jnp.dot(
        se[...], spread, preferred_element_type=jnp.float32, precision=lax.Precision.HIGHEST
    )

    for index in seq_others:
        arrived(factors.at[index], f_recv.at[index])
        arrived(xs.at[index], x_recv.at[index])
    wide = xs[...].astype(jnp.float32).reshape(tokens, features)
    factor = factors[...].reshape(tokens, 128)[:, :1]
    normed[...] = (wide * factor * gain[...]).astype(jnp.bfloat16)

    for step in range(chans):
        w_in_copies[step].wait()
        terms = contract_last(normed[...], w_in[step].reshape(3 * block, features))
        if step < seqs:
            fetch_out(step)
        if step == chans - 1:
            for part in range(3):
                own[part] = terms[:, part * block : (part + 1) * block]
            continue
        for part in range(3):
            stage[step, part] = terms[:, part * block : (part + 1) * block].astype(jnp.bfloat16)
        sent.append(send(
            stage.at[step], landed.at[chan],
            p_send.at[step], p_recv.at[chan], "chan", chan_others[step],
        ))
    for step in range(len(w_out_copies), seqs):
        fetch_out(step)

    mine = pl.ds(pl.multiple_of(chan * block, block), block)
    for index in reversed(chan_others):
        arrived(landed.at[index], p_recv.at[index])
    featured = []
    for part in range(3):
        value = own[part]
        for index in reversed(chan_others):
            value += landed[index, part].astype(jnp.float32)
        featured.append(sum(
            short[lag, part : part + 1, mine] * delayed(value, lag) for lag in range(3)
        ))
    product = featured[1] * featured[2]
    filtered = sum(long_taps[lag : lag + 1] * delayed(product, lag) for lag in range(7))
    gathered[seq] = (featured[0] * filtered).astype(jnp.bfloat16)
    sent += [
        send(gathered.at[seq], gathered.at[seq], g_send.at[step], g_recv.at[seq], "seq", index)
        for step, index in reversed(list(enumerate(seq_others)))
    ]

    for step, index in enumerate(out_order):
        w_out_copies[step].wait()
        if step > 0:
            arrived(gathered.at[index], g_recv.at[index])
        terms = contract_last(gathered[index], w_out[step])
        if step == 0:
            total[...] = terms
        else:
            total[...] += terms
    leaving[...] = total[...].reshape(leaving.shape).astype(jnp.bfloat16)
    sent += [
        send(leaving.at[index], arriving.at[chan], o_send.at[step], o_recv.at[chan], "chan", index)
        for step, index in enumerate(chan_others)
    ]
    result = total[pl.ds(pl.multiple_of(chan * rows, rows), rows)]
    for index in reversed(chan_others):
        arrived(arriving.at[index], o_recv.at[index])
        result += arriving[index].astype(jnp.float32)
    out_ref[...] = result
    for copy in sent:
        copy.wait_send()


def shards(seqs, chans, x_tokens, norm_gain, w_in, short_filter, se_filter, w_out):
    held, features = x_tokens.shape
    columns = w_in.shape[1]
    tokens, block, rows = held * seqs, columns // chans, held * seqs // chans
    weight_bytes = 2 * (w_in.size + w_out.size // chans)
    if (
        seqs < 2 or chans < 2 or held % 8 or rows % 8 or tokens != rows * chans or tokens > 256
        or block * chans != columns or block % 128 or features % 128 or weight_bytes > 40 * MIB
    ):
        return plain(x_tokens, norm_gain, w_in, short_filter, se_filter, w_out)
    bf16, f32 = jnp.bfloat16, jnp.float32
    dma = pltpu.SemaphoreType.DMA
    anywhere = pl.BlockSpec(memory_space=pl.ANY)
    result = pl.pallas_call(
        functools.partial(kernel, seqs, chans),
        out_shape=jax.ShapeDtypeStruct((rows, columns), f32),
        in_specs=[anywhere] * 6,
        out_specs=pl.BlockSpec(memory_space=pltpu.VMEM),
        scratch_shapes=[
            pltpu.VMEM((seqs, held, features), bf16),
            pltpu.VMEM((1, features), f32),
            pltpu.VMEM((chans, 3, block, features), bf16),
            pltpu.VMEM(short_filter.shape, f32),
            pltpu.VMEM(se_filter.shape, f32),
            pltpu.VMEM((seqs, columns, block), bf16),
            pltpu.VMEM((tokens, features), bf16),
            pltpu.VMEM((chans, held, 128), f32),
            pltpu.VMEM((seqs, held, 128), f32),
            pltpu.VMEM((chans - 1, 3, tokens, block), bf16),
            pltpu.VMEM((chans, 3, tokens, block), bf16),
            pltpu.VMEM((3, tokens, block), f32),
            pltpu.VMEM((seqs, tokens, block), bf16),
            pltpu.VMEM((tokens, columns), f32),
            pltpu.VMEM((chans, rows, columns), bf16),
            pltpu.VMEM((chans, rows, columns), bf16),
            dma((4,)), dma((chans,)), dma((seqs,)),
            dma((seqs - 1,)), dma((seqs,)),
            dma((chans - 1,)), dma((chans,)),
            dma((seqs - 1,)), dma((seqs,)),
            dma((chans - 1,)), dma((chans,)),
            dma((seqs - 1,)), dma((seqs,)),
            dma((chans - 1,)), dma((chans,)),
        ],
        compiler_params=pltpu.CompilerParams(
            collective_id=0, has_side_effects=True, vmem_limit_bytes=60 * MIB
        ),
        cost_estimate=pl.CostEstimate(
            flops=tokens * weight_bytes, bytes_accessed=weight_bytes, transcendentals=0
        ),
    )(x_tokens, norm_gain.reshape(1, features), w_in, short_filter, se_filter, w_out)
    return result.astype(bf16)


def solution(mesh):
    placed = (
        P(("parts", "seq"), "chan"),
        P("chan"),
        P(None, "seq", "chan"),
        P(None, None, "seq"),
        P(None, "seq"),
        P("seq", None),
    )
    return jax.shard_map(
        functools.partial(shards, mesh.shape["seq"], mesh.shape["chan"]),
        mesh=mesh, in_specs=placed, out_specs=P(("parts", "chan"), "seq"), check_vma=False,
    )
```

```python
import functools

import jax
import jax.numpy as jnp
from jax import lax
from jax.experimental import pallas as pl
from jax.experimental.pallas import tpu as pltpu
from jax.sharding import PartitionSpec as P

D = 8192
GROUP = 16
MIB = 2**20


epsilon = 1e-06


def from_behind(value, axis, steps):
    count = lax.axis_size(axis)
    leading, last = (max(0, -steps), min(count, count - steps))
    return lax.ppermute(value, axis, [(source, source + steps) for source in range(leading, last)])


def mixer(extended, short_taps, long_taps):
    wide = extended.astype(jnp.float32)
    row_count = wide.shape[0]
    featured = sum(
        (short_taps[offset] * wide[2 - offset : row_count - offset] for offset in range(3))
    )
    queries = featured[:, 0]
    product = featured[:, 1] * featured[:, 2]
    length = product.shape[0]
    filtered = sum(
        (long_taps[offset] * product[6 - offset : length - offset] for offset in range(7))
    )
    return (queries[6:] * filtered).astype(jnp.bfloat16)


def contract_last(left, right):
    return lax.dot_general(
        left, right, (((1,), (1,)), ((), ())), preferred_element_type=jnp.float32
    )


def plain(x_tokens, norm_gain, w_in, short_filter, se_filter, w_out):
    wide = x_tokens.astype(jnp.float32)
    local_squares = jnp.sum(wide * wide, axis=1, keepdims=True)
    total_squares = lax.psum(local_squares, "chan")
    factor = lax.rsqrt(total_squares / D + epsilon)
    normed = (wide * factor * norm_gain).astype(jnp.bfloat16)
    columns = w_in.shape[1]
    flat_in = w_in.reshape(3 * columns, w_in.shape[2])
    piece = lax.all_gather(normed, "seq", axis=0, tiled=True)
    partial_terms = contract_last(piece, flat_in).reshape(piece.shape[0], 3, columns)
    long_full = jnp.repeat(se_filter, GROUP, axis=1)
    mine = lax.psum_scatter(partial_terms, "chan", scatter_dimension=0, tiled=True).astype(
        jnp.bfloat16
    )
    previous = from_behind(mine[-8:], "chan", 1)
    extended = jnp.concatenate([previous, mine], axis=0)
    gated = mixer(extended, short_filter, long_full)
    result = contract_last(lax.all_gather(gated, "seq", axis=1, tiled=True), w_out)
    return result.astype(jnp.bfloat16)


def partners(me, count):
    if count % 2:
        return [lax.rem(me + step, count) for step in range(1, count)]
    chip, core, chips = me // 2, lax.rem(me, 2), count // 2
    found = []
    for step in range(1, chips):
        other = 2 * lax.rem(chip + step, chips)
        found += [other + core, other + 1 - core]
    return found + [2 * chip + 1 - core]


def nearest_first(me, count):
    found = partners(me, count)
    return found if count % 2 else found[-1:] + found[:-1]


def delayed(value, steps):
    if steps == 0:
        return value
    tokens = lax.broadcasted_iota(jnp.int32, value.shape, 0)
    return jnp.where(tokens >= steps, pltpu.roll(value, steps, 0), 0.0)


def kernel(
    seqs, chans,
    x_hbm, gain_hbm, w_in_hbm, short_hbm, se_hbm, w_out_hbm, out_ref,
    xs, gain, w_in, short, se, w_out, normed, squares, factors, stage, landed, own, gathered, total,
    leaving, arriving,
    small_sem, w_in_sem, w_out_sem, x_send, x_recv, sq_send, sq_recv, f_send, f_recv, p_send, p_recv,
    g_send, g_recv, o_send, o_recv,
):
    seq, chan = lax.axis_index("seq"), lax.axis_index("chan")
    tokens, block = own.shape[1:]
    columns, features = w_out.shape[1], w_in.shape[3]
    rows = out_ref.shape[0]
    seq_others = nearest_first(seq, seqs)
    chan_others = partners(chan, chans)

    def send(source, target, send_sem, recv_sem, axis, index):
        copy = pltpu.make_async_remote_copy(
            src_ref=source, dst_ref=target, send_sem=send_sem, recv_sem=recv_sem,
            device_id={axis: index}, device_id_type=pl.DeviceIdType.MESH,
        )
        copy.start()
        return copy

    def local(source, target, sem):
        copy = pltpu.make_async_copy(source, target, sem)
        copy.start()
        return copy

    def arrived(target, sem):
        pltpu.make_async_copy(target, target, sem).wait()

    x_copy = local(x_hbm, xs.at[seq], small_sem.at[0])
    gain_copy = local(gain_hbm, gain, small_sem.at[1])
    short_copy = local(short_hbm, short, small_sem.at[2])
    se_copy = local(se_hbm, se, small_sem.at[3])
    w_in_copies, w_out_copies = [], []

    def fetch_in(step):
        span = pl.ds(pl.multiple_of(in_order[step] * block, block), block)
        w_in_copies.append(local(
            w_in_hbm.at[:, span], w_in.at[step], w_in_sem.at[step]
        ))

    def fetch_out(step):
        span = pl.ds(pl.multiple_of(out_order[step] * columns + chan * block, block), block)
        w_out_copies.append(local(w_out_hbm.at[:, span], w_out.at[step], w_out_sem.at[step]))

    in_order, out_order = chan_others + [chan], [seq] + seq_others
    for step in range(chans // 2):
        fetch_in(step)

    barrier = pltpu.get_barrier_semaphore()
    for axis, others in (("seq", seq_others), ("chan", chan_others)):
        for index in others:
            pl.semaphore_signal(
                barrier, inc=1, device_id={axis: index}, device_id_type=pl.DeviceIdType.MESH
            )
    x_copy.wait()
    wide = xs[seq].astype(jnp.float32)
    squares[chan] = jnp.broadcast_to(
        jnp.sum(wide * wide, axis=1, keepdims=True), squares.shape[1:]
    )
    pl.semaphore_wait(barrier, seqs + chans - 2)

    sent = [
        send(squares.at[chan], squares.at[chan], sq_send.at[step], sq_recv.at[chan], "chan", index)
        for step, index in enumerate(chan_others)
    ]
    sent += [
        send(xs.at[seq], xs.at[seq], x_send.at[step], x_recv.at[seq], "seq", index)
        for step, index in reversed(list(enumerate(seq_others)))
    ]

    for index in chan_others:
        arrived(squares.at[index], sq_recv.at[index])
    factors[seq] = lax.rsqrt(jnp.sum(squares[...], axis=0) / (features * chans) + epsilon)
    sent += [
        send(factors.at[seq], factors.at[seq], f_send.at[step], f_recv.at[seq], "seq", index)
        for step, index in reversed(list(enumerate(seq_others)))
    ]

    for step in range(len(w_in_copies), chans):
        fetch_in(step)

    se_copy.wait()
    short_copy.wait()
    gain_copy.wait()
    filters = se.shape[1]
    group = columns // filters
    first = lax.broadcasted_iota(jnp.int32, (filters, block), 0) * group
    channel = lax.broadcasted_iota(jnp.int32, (filters, block), 1) + chan * block
    spread = jnp.where((channel >= first) & (channel < first + group), 1.0, 0.0)
    long_taps = jnp.dot(
        se[...], spread, preferred_element_type=jnp.float32, precision=lax.Precision.HIGHEST
    )

    for index in seq_others:
        arrived(factors.at[index], f_recv.at[index])
        arrived(xs.at[index], x_recv.at[index])
    wide = xs[...].astype(jnp.float32).reshape(tokens, features)
    factor = factors[...].reshape(tokens, 128)[:, :1]
    normed[...] = (wide * factor * gain[...]).astype(jnp.bfloat16)

    for step in range(chans):
        w_in_copies[step].wait()
        terms = contract_last(normed[...], w_in[step].reshape(3 * block, features))
        if step < seqs:
            fetch_out(step)
        if step == chans - 1:
            for part in range(3):
                own[part] = terms[:, part * block : (part + 1) * block]
            continue
        for part in range(3):
            stage[step, part] = terms[:, part * block : (part + 1) * block].astype(jnp.bfloat16)
        sent.append(send(
            stage.at[step], landed.at[chan],
            p_send.at[step], p_recv.at[chan], "chan", chan_others[step],
        ))
    for step in range(len(w_out_copies), seqs):
        fetch_out(step)

    mine = pl.ds(pl.multiple_of(chan * block, block), block)
    for index in reversed(chan_others):
        arrived(landed.at[index], p_recv.at[index])
    featured = []
    for part in range(3):
        value = own[part]
        for index in reversed(chan_others):
            value += landed[index, part].astype(jnp.float32)
        featured.append(sum(
            short[lag, part : part + 1, mine] * delayed(value, lag) for lag in range(3)
        ))
    product = featured[1] * featured[2]
    filtered = sum(long_taps[lag : lag + 1] * delayed(product, lag) for lag in range(7))
    gathered[seq] = (featured[0] * filtered).astype(jnp.bfloat16)
    sent += [
        send(gathered.at[seq], gathered.at[seq], g_send.at[step], g_recv.at[seq], "seq", index)
        for step, index in reversed(list(enumerate(seq_others)))
    ]

    for step, index in enumerate(out_order):
        w_out_copies[step].wait()
        if step > 0:
            arrived(gathered.at[index], g_recv.at[index])
        terms = contract_last(gathered[index], w_out[step])
        if step == 0:
            total[...] = terms
        else:
            total[...] += terms
    leaving[...] = total[...].reshape(leaving.shape).astype(jnp.bfloat16)
    sent += [
        send(leaving.at[index], arriving.at[chan], o_send.at[step], o_recv.at[chan], "chan", index)
        for step, index in enumerate(chan_others)
    ]
    result = total[pl.ds(pl.multiple_of(chan * rows, rows), rows)]
    for index in reversed(chan_others):
        arrived(arriving.at[index], o_recv.at[index])
        result += arriving[index].astype(jnp.float32)
    out_ref[...] = result.astype(jnp.bfloat16)
    for copy in sent:
        copy.wait_send()


def shards(seqs, chans, x_tokens, norm_gain, w_in, short_filter, se_filter, w_out):
    held, features = x_tokens.shape
    columns = w_in.shape[1]
    tokens, block, rows = held * seqs, columns // chans, held * seqs // chans
    weight_bytes = 2 * (w_in.size + w_out.size // chans)
    if (
        seqs < 2 or chans < 2 or held % 8 or rows % 8 or tokens != rows * chans or tokens > 256
        or block * chans != columns or block % 128 or features % 128 or weight_bytes > 40 * MIB
    ):
        return plain(x_tokens, norm_gain, w_in, short_filter, se_filter, w_out)
    bf16, f32 = jnp.bfloat16, jnp.float32
    dma = pltpu.SemaphoreType.DMA
    anywhere = pl.BlockSpec(memory_space=pl.ANY)
    return pl.pallas_call(
        functools.partial(kernel, seqs, chans),
        out_shape=jax.ShapeDtypeStruct((rows, columns), bf16),
        in_specs=[anywhere] * 6,
        out_specs=pl.BlockSpec(memory_space=pltpu.VMEM),
        scratch_shapes=[
            pltpu.VMEM((seqs, held, features), bf16),
            pltpu.VMEM((1, features), f32),
            pltpu.VMEM((chans, 3, block, features), bf16),
            pltpu.VMEM(short_filter.shape, f32),
            pltpu.VMEM(se_filter.shape, f32),
            pltpu.VMEM((seqs, columns, block), bf16),
            pltpu.VMEM((tokens, features), bf16),
            pltpu.VMEM((chans, held, 128), f32),
            pltpu.VMEM((seqs, held, 128), f32),
            pltpu.VMEM((chans - 1, 3, tokens, block), bf16),
            pltpu.VMEM((chans, 3, tokens, block), bf16),
            pltpu.VMEM((3, tokens, block), f32),
            pltpu.VMEM((seqs, tokens, block), bf16),
            pltpu.VMEM((tokens, columns), f32),
            pltpu.VMEM((chans, rows, columns), bf16),
            pltpu.VMEM((chans, rows, columns), bf16),
            dma((4,)), dma((chans,)), dma((seqs,)),
            dma((seqs - 1,)), dma((seqs,)),
            dma((chans - 1,)), dma((chans,)),
            dma((seqs - 1,)), dma((seqs,)),
            dma((chans - 1,)), dma((chans,)),
            dma((seqs - 1,)), dma((seqs,)),
            dma((chans - 1,)), dma((chans,)),
        ],
        compiler_params=pltpu.CompilerParams(
            collective_id=0, has_side_effects=True, vmem_limit_bytes=60 * MIB
        ),
        cost_estimate=pl.CostEstimate(
            flops=tokens * weight_bytes, bytes_accessed=weight_bytes, transcendentals=0
        ),
    )(x_tokens, norm_gain.reshape(1, features), w_in, short_filter, se_filter, w_out)


def solution(mesh):
    placed = (
        P(("parts", "seq"), "chan"),
        P("chan"),
        P(None, "seq", "chan"),
        P(None, None, "seq"),
        P(None, "seq"),
        P("seq", None),
    )
    return jax.shard_map(
        functools.partial(shards, mesh.shape["seq"], mesh.shape["chan"]),
        mesh=mesh, in_specs=placed, out_specs=P(("parts", "chan"), "seq"), check_vma=False,
    )
```

```python
import functools

import jax
import jax.numpy as jnp
from jax import lax
from jax.experimental import pallas as pl
from jax.experimental.pallas import tpu as pltpu
from jax.sharding import PartitionSpec as P

D = 8192
GROUP = 16
MIB = 2**20


epsilon = 1e-06


def from_behind(value, axis, steps):
    count = lax.axis_size(axis)
    leading, last = (max(0, -steps), min(count, count - steps))
    return lax.ppermute(value, axis, [(source, source + steps) for source in range(leading, last)])


def mixer(extended, short_taps, long_taps):
    wide = extended.astype(jnp.float32)
    row_count = wide.shape[0]
    featured = sum(
        (short_taps[offset] * wide[2 - offset : row_count - offset] for offset in range(3))
    )
    queries = featured[:, 0]
    product = featured[:, 1] * featured[:, 2]
    length = product.shape[0]
    filtered = sum(
        (long_taps[offset] * product[6 - offset : length - offset] for offset in range(7))
    )
    return (queries[6:] * filtered).astype(jnp.bfloat16)


def contract_last(left, right):
    return lax.dot_general(
        left, right, (((1,), (1,)), ((), ())), preferred_element_type=jnp.float32
    )


def plain(x_tokens, norm_gain, w_in, short_filter, se_filter, w_out):
    wide = x_tokens.astype(jnp.float32)
    local_squares = jnp.sum(wide * wide, axis=1, keepdims=True)
    total_squares = lax.psum(local_squares, "chan")
    factor = lax.rsqrt(total_squares / D + epsilon)
    normed = (wide * factor * norm_gain).astype(jnp.bfloat16)
    columns = w_in.shape[1]
    flat_in = w_in.reshape(3 * columns, w_in.shape[2])
    piece = lax.all_gather(normed, "seq", axis=0, tiled=True)
    partial_terms = contract_last(piece, flat_in).reshape(piece.shape[0], 3, columns)
    long_full = jnp.repeat(se_filter, GROUP, axis=1)
    mine = lax.psum_scatter(partial_terms, "chan", scatter_dimension=0, tiled=True).astype(
        jnp.bfloat16
    )
    previous = from_behind(mine[-8:], "chan", 1)
    extended = jnp.concatenate([previous, mine], axis=0)
    gated = mixer(extended, short_filter, long_full)
    result = contract_last(lax.all_gather(gated, "seq", axis=1, tiled=True), w_out)
    return result.astype(jnp.bfloat16)


def partners(me, count):
    if count % 2:
        return [lax.rem(me + step, count) for step in range(1, count)]
    chip, core, chips = me // 2, lax.rem(me, 2), count // 2
    found = []
    for step in range(1, chips):
        other = 2 * lax.rem(chip + step, chips)
        found += [other + core, other + 1 - core]
    return found + [2 * chip + 1 - core]


def nearest_first(me, count):
    found = partners(me, count)
    return found if count % 2 else found[-1:] + found[:-1]


def delayed(value, steps):
    if steps == 0:
        return value
    tokens = lax.broadcasted_iota(jnp.int32, value.shape, 0)
    return jnp.where(tokens >= steps, pltpu.roll(value, steps, 0), 0.0)


def kernel(
    seqs, chans,
    x_hbm, gain_hbm, w_in_hbm, short_hbm, se_hbm, w_out_hbm, out_ref,
    xs, gain, w_in, short, se, w_out, normed, squares, factors, stage, landed, own, gathered, total,
    leaving, arriving,
    small_sem, w_in_sem, w_out_sem, x_send, x_recv, sq_send, sq_recv, f_send, f_recv, p_send, p_recv,
    g_send, g_recv, o_send, o_recv,
):
    seq, chan = lax.axis_index("seq"), lax.axis_index("chan")
    tokens, block = own.shape[1:]
    columns, features = w_out.shape[1], w_in.shape[3]
    rows = out_ref.shape[0]
    seq_others = nearest_first(seq, seqs)
    chan_others = partners(chan, chans)

    def send(source, target, send_sem, recv_sem, axis, index):
        copy = pltpu.make_async_remote_copy(
            src_ref=source, dst_ref=target, send_sem=send_sem, recv_sem=recv_sem,
            device_id={axis: index}, device_id_type=pl.DeviceIdType.MESH,
        )
        copy.start()
        return copy

    def local(source, target, sem):
        copy = pltpu.make_async_copy(source, target, sem)
        copy.start()
        return copy

    def arrived(target, sem):
        pltpu.make_async_copy(target, target, sem).wait()

    x_copy = local(x_hbm, xs.at[seq], small_sem.at[0])
    gain_copy = local(gain_hbm, gain, small_sem.at[1])
    short_copy = local(short_hbm, short, small_sem.at[2])
    se_copy = local(se_hbm, se, small_sem.at[3])
    w_in_copies, w_out_copies = [], []

    def fetch_in(step):
        span = pl.ds(pl.multiple_of(in_order[step] * block, block), block)
        w_in_copies.append(local(
            w_in_hbm.at[:, span], w_in.at[step], w_in_sem.at[step]
        ))

    def fetch_out(step):
        span = pl.ds(pl.multiple_of(out_order[step] * columns + chan * block, block), block)
        w_out_copies.append(local(w_out_hbm.at[:, span], w_out.at[step], w_out_sem.at[step]))

    in_order, out_order = chan_others + [chan], [seq] + seq_others
    for step in range(chans):
        fetch_in(step)
    for step in range(seqs):
        fetch_out(step)

    barrier = pltpu.get_barrier_semaphore()
    for axis, others in (("seq", seq_others), ("chan", chan_others)):
        for index in others:
            pl.semaphore_signal(
                barrier, inc=1, device_id={axis: index}, device_id_type=pl.DeviceIdType.MESH
            )
    x_copy.wait()
    wide = xs[seq].astype(jnp.float32)
    squares[chan] = jnp.broadcast_to(
        jnp.sum(wide * wide, axis=1, keepdims=True), squares.shape[1:]
    )
    pl.semaphore_wait(barrier, seqs + chans - 2)

    sent = [
        send(squares.at[chan], squares.at[chan], sq_send.at[step], sq_recv.at[chan], "chan", index)
        for step, index in enumerate(chan_others)
    ]
    sent += [
        send(xs.at[seq], xs.at[seq], x_send.at[step], x_recv.at[seq], "seq", index)
        for step, index in reversed(list(enumerate(seq_others)))
    ]

    for index in chan_others:
        arrived(squares.at[index], sq_recv.at[index])
    factors[seq] = lax.rsqrt(jnp.sum(squares[...], axis=0) / (features * chans) + epsilon)
    sent += [
        send(factors.at[seq], factors.at[seq], f_send.at[step], f_recv.at[seq], "seq", index)
        for step, index in reversed(list(enumerate(seq_others)))
    ]

    se_copy.wait()
    short_copy.wait()
    gain_copy.wait()
    filters = se.shape[1]
    group = columns // filters
    first = lax.broadcasted_iota(jnp.int32, (filters, block), 0) * group
    channel = lax.broadcasted_iota(jnp.int32, (filters, block), 1) + chan * block
    spread = jnp.where((channel >= first) & (channel < first + group), 1.0, 0.0)
    long_taps = jnp.dot(
        se[...], spread, preferred_element_type=jnp.float32, precision=lax.Precision.HIGHEST
    )

    for index in seq_others:
        arrived(factors.at[index], f_recv.at[index])
        arrived(xs.at[index], x_recv.at[index])
    wide = xs[...].astype(jnp.float32).reshape(tokens, features)
    factor = factors[...].reshape(tokens, 128)[:, :1]
    normed[...] = (wide * factor * gain[...]).astype(jnp.bfloat16)

    for step in range(chans):
        w_in_copies[step].wait()
        terms = contract_last(normed[...], w_in[step].reshape(3 * block, features))
        if step == chans - 1:
            for part in range(3):
                own[part] = terms[:, part * block : (part + 1) * block]
            continue
        for part in range(3):
            stage[step, part] = terms[:, part * block : (part + 1) * block].astype(jnp.bfloat16)
        sent.append(send(
            stage.at[step], landed.at[chan],
            p_send.at[step], p_recv.at[chan], "chan", chan_others[step],
        ))

    mine = pl.ds(pl.multiple_of(chan * block, block), block)
    for index in reversed(chan_others):
        arrived(landed.at[index], p_recv.at[index])
    featured = []
    for part in range(3):
        value = own[part]
        for index in reversed(chan_others):
            value += landed[index, part].astype(jnp.float32)
        featured.append(sum(
            short[lag, part : part + 1, mine] * delayed(value, lag) for lag in range(3)
        ))
    product = featured[1] * featured[2]
    filtered = sum(long_taps[lag : lag + 1] * delayed(product, lag) for lag in range(7))
    gathered[seq] = (featured[0] * filtered).astype(jnp.bfloat16)
    sent += [
        send(gathered.at[seq], gathered.at[seq], g_send.at[step], g_recv.at[seq], "seq", index)
        for step, index in reversed(list(enumerate(seq_others)))
    ]

    for step, index in enumerate(out_order):
        w_out_copies[step].wait()
        if step > 0:
            arrived(gathered.at[index], g_recv.at[index])
        terms = contract_last(gathered[index], w_out[step])
        if step == 0:
            total[...] = terms
        else:
            total[...] += terms
    leaving[...] = total[...].reshape(leaving.shape).astype(jnp.bfloat16)
    sent += [
        send(leaving.at[index], arriving.at[chan], o_send.at[step], o_recv.at[chan], "chan", index)
        for step, index in enumerate(chan_others)
    ]
    result = total[pl.ds(pl.multiple_of(chan * rows, rows), rows)]
    for index in reversed(chan_others):
        arrived(arriving.at[index], o_recv.at[index])
        result += arriving[index].astype(jnp.float32)
    out_ref[...] = result.astype(jnp.bfloat16)
    for copy in sent:
        copy.wait_send()


def shards(seqs, chans, x_tokens, norm_gain, w_in, short_filter, se_filter, w_out):
    held, features = x_tokens.shape
    columns = w_in.shape[1]
    tokens, block, rows = held * seqs, columns // chans, held * seqs // chans
    weight_bytes = 2 * (w_in.size + w_out.size // chans)
    if (
        seqs < 2 or chans < 2 or held % 8 or rows % 8 or tokens != rows * chans or tokens > 256
        or block * chans != columns or block % 128 or features % 128 or weight_bytes > 40 * MIB
    ):
        return plain(x_tokens, norm_gain, w_in, short_filter, se_filter, w_out)
    bf16, f32 = jnp.bfloat16, jnp.float32
    dma = pltpu.SemaphoreType.DMA
    anywhere = pl.BlockSpec(memory_space=pl.ANY)
    return pl.pallas_call(
        functools.partial(kernel, seqs, chans),
        out_shape=jax.ShapeDtypeStruct((rows, columns), bf16),
        in_specs=[anywhere] * 6,
        out_specs=pl.BlockSpec(memory_space=pltpu.VMEM),
        scratch_shapes=[
            pltpu.VMEM((seqs, held, features), bf16),
            pltpu.VMEM((1, features), f32),
            pltpu.VMEM((chans, 3, block, features), bf16),
            pltpu.VMEM(short_filter.shape, f32),
            pltpu.VMEM(se_filter.shape, f32),
            pltpu.VMEM((seqs, columns, block), bf16),
            pltpu.VMEM((tokens, features), bf16),
            pltpu.VMEM((chans, held, 128), f32),
            pltpu.VMEM((seqs, held, 128), f32),
            pltpu.VMEM((chans - 1, 3, tokens, block), bf16),
            pltpu.VMEM((chans, 3, tokens, block), bf16),
            pltpu.VMEM((3, tokens, block), f32),
            pltpu.VMEM((seqs, tokens, block), bf16),
            pltpu.VMEM((tokens, columns), f32),
            pltpu.VMEM((chans, rows, columns), bf16),
            pltpu.VMEM((chans, rows, columns), bf16),
            dma((4,)), dma((chans,)), dma((seqs,)),
            dma((seqs - 1,)), dma((seqs,)),
            dma((chans - 1,)), dma((chans,)),
            dma((seqs - 1,)), dma((seqs,)),
            dma((chans - 1,)), dma((chans,)),
            dma((seqs - 1,)), dma((seqs,)),
            dma((chans - 1,)), dma((chans,)),
        ],
        compiler_params=pltpu.CompilerParams(
            collective_id=0, has_side_effects=True, vmem_limit_bytes=60 * MIB
        ),
        cost_estimate=pl.CostEstimate(
            flops=tokens * weight_bytes, bytes_accessed=weight_bytes, transcendentals=0
        ),
    )(x_tokens, norm_gain.reshape(1, features), w_in, short_filter, se_filter, w_out)


def solution(mesh):
    placed = (
        P(("parts", "seq"), "chan"),
        P("chan"),
        P(None, "seq", "chan"),
        P(None, None, "seq"),
        P(None, "seq"),
        P("seq", None),
    )
    return jax.shard_map(
        functools.partial(shards, mesh.shape["seq"], mesh.shape["chan"]),
        mesh=mesh, in_specs=placed, out_specs=P(("parts", "chan"), "seq"), check_vma=False,
    )
```
